512 devices in a mesh: section: 16 (over z, core), tensor: 32 (over y, x).
Axes of the slice: x: 4, y: 8, z: 8, core: 2. Of those that a mesh axis runs over, the one named last changes fastest.
Arguments:
- resid: bfloat16 [128, 3584], P('tensor'), may hold values from -6 to 6
- w_enc: bfloat16 [114688, 3584], P(('section', 'tensor')), may hold values from -0.09375 to 0.09375
- b_enc: float32 [114688], P(('section', 'tensor')), may hold values from -1 to 0.5
- w_dec: bfloat16 [114688, 3584], P(('section', 'tensor')), may hold values from -0.015625 to 0.015625
- b_dec: float32 [3584], replicated, may hold values from -3 to 3
Outputs:
- recon: float32 [128, 3584], P('tensor')
- grad_w_dec: bfloat16 [114688, 3584], P(('section', 'tensor'))
- code_grad: float32 [128, 114688], P(None, ('section', 'tensor'))
- grad_b_dec: float32 [3584], replicated
- loss_value: float32 [], replicated
The draws below stay inside these ranges and needn't reach their ends.
All inputs are finite; a program needn't handle non-finite values.
Results may differ from the reference program's by a relative error of at most 0.0032.
The reference program's roundings to bfloat16 on the way (of `codes` and `err_half`) count: a program that leaves them out, or rounds other values in their place, can miss the bound.
Values may be sent and summed in bfloat16 or wider, within the bound.
A program may use at most 64 MiB of HBM per device.

```python
import jax
import jax.numpy as jnp
from jax import lax

D = 3584
LAT_DEV = 224
ROWS = 128
LATENTS = 114688
N_SECTION = 16
N_TENSOR = 32


def block_levels(rng, extent, split, low, high):
    loudness, own = 1.0, jax.random.fold_in(rng, 6)
    for dim, blocks in split:
        steps = jnp.exp(jax.random.uniform(jax.random.fold_in(own, dim), (blocks,), jnp.float32, low / len(split), high / len(split)))
        loudness = loudness * jnp.repeat(steps, extent[dim] // blocks).reshape([-1 if axis == dim else 1 for axis in range(len(extent))])
    return loudness


def bell_draw(rng, dims, width, limit, shards=(), held_as=jnp.bfloat16):
    gain = block_levels(rng, dims, shards, -0.22, 0.18) if shards else 1.0
    result = jax.random.normal(rng, dims, jnp.float32) * width * gain
    return jnp.minimum(jnp.maximum(result, -limit), limit).astype(held_as)


def setup_inputs(seed: int = 0) -> dict:
    seeds = jax.random.split(jax.random.key(seed), 6)
    resid = bell_draw(seeds[0], (ROWS, D), 1.0, 6.0, ((0, 32),))
    w_enc = bell_draw(seeds[1], (LATENTS, D), D ** -0.5, 0.09375, ((0, 512),))
    b_enc = jnp.clip(-1.0 + 1.5 * jax.random.uniform(seeds[2], (LATENTS,), jnp.float32) ** block_levels(seeds[2], (LATENTS,), ((0, 512),), -0.2, 0.2), -1.0, 0.5)
    w_dec = bell_draw(seeds[3], (LATENTS, D), LATENTS ** -0.5, 0.015625, ((0, 512),))
    b_dec = bell_draw(seeds[4], (D,), 0.5, 3.0, (), jnp.float32)
    return dict(resid=resid, w_enc=w_enc, b_enc=b_enc, w_dec=w_dec, b_dec=b_dec)


epsilon = 1e-06

def block_codes(resid, enc_block, bias_block):
    preact = lax.dot_general(resid, enc_block, (((1,), (1,)), ((), ())), preferred_element_type=jnp.float32) + bias_block
    return jnp.maximum(preact, 0.0).astype(jnp.bfloat16)

def block_norm(dec_block):
    dec_f32 = dec_block.astype(jnp.float32)
    return (dec_f32, jnp.sqrt(lax.optimization_barrier(jnp.sum(dec_f32 * dec_f32, axis=1)) + epsilon))

def reference(resid, w_enc, b_enc, w_dec, b_dec):
    blocks = N_SECTION * N_TENSOR
    enc_blocks = w_enc.reshape(blocks, LAT_DEV, D)
    bias_blocks = b_enc.reshape(blocks, LAT_DEV)
    dec_blocks = w_dec.reshape(blocks, LAT_DEV, D)

    def forward(carry, pieces):
        enc_block, bias_block, dec_block = pieces
        codes = block_codes(resid, enc_block, bias_block)
        dec_f32, dec_norm = block_norm(dec_block)
        total, penalty = carry
        total = total + jnp.dot(codes, dec_block, preferred_element_type=jnp.float32)
        penalty = penalty + jnp.sum(codes.astype(jnp.float32) * dec_norm)
        return ((total, penalty), None)
    start = (jnp.zeros((ROWS, D), jnp.float32), jnp.zeros((), jnp.float32))
    (summed, penalty), unused = lax.scan(forward, start, (enc_blocks, bias_blocks, dec_blocks))
    recon = summed + b_dec
    errors = recon - resid.astype(jnp.float32)
    loss_value = (0.5 * jnp.sum(errors * errors) + penalty) / (ROWS * D)
    err_half = errors.astype(jnp.bfloat16)

    def backward(pieces):
        enc_block, bias_block, dec_block = pieces
        codes = block_codes(resid, enc_block, bias_block)
        dec_f32, dec_norm = block_norm(dec_block)
        code_sums = lax.optimization_barrier(jnp.sum(codes.astype(jnp.float32), axis=0))
        grad_block = lax.dot_general(codes, err_half, (((0,), (0,)), ((), ())), preferred_element_type=jnp.float32)
        grad_block = grad_block + code_sums[:, None] * dec_f32 / dec_norm[:, None]
        code_block = lax.dot_general(err_half, dec_block, (((1,), (1,)), ((), ())), preferred_element_type=jnp.float32) + dec_norm
        return (grad_block.astype(jnp.bfloat16), code_block)
    grad_blocks, code_blocks = lax.map(backward, (enc_blocks, bias_blocks, dec_blocks))
    grad_w_dec = grad_blocks.reshape(LATENTS, D)
    code_grad = jnp.transpose(code_blocks, (1, 0, 2)).reshape(ROWS, LATENTS)
    grad_b_dec = lax.optimization_barrier(jnp.sum(errors, axis=0))
    return (recon, grad_w_dec, code_grad, grad_b_dec, loss_value)
```

```python
import functools

import jax
import jax.numpy as jnp
from jax import lax
from jax.experimental import pallas as pl
from jax.experimental.pallas import tpu as pltpu
from jax.sharding import PartitionSpec as P

MESH = pl.DeviceIdType.MESH
F32, BF16 = jnp.float32, jnp.bfloat16
epsilon = 1e-06

NX, NY, NZ = 4, 8, 8
D, LAT, ROWS = 3584, 224, 128
HALF, Q = D // 2, D // 4
SCALE = 1.0 / (ROWS * D)
NEAR = (1, 7, 2, 6, 3, 5, 4)
FAR = (4, 3, 5, 2, 6, 1, 7)


def far_step(n):
    return 4 + (1 - 2 * (n % 2)) * ((n + 1) // 2)


def near_step(n):
    return (1 - 2 * (n % 2)) * ((n + 2) // 2) + 8 * (n % 2)


def kernel(
    resid, wenc, benc, wdec, bdec,
    recon_o, gw_o, cg_o, gb_o, loss_o,
    rg, we, wd, wds, bs, lhs, px, pr, cc, part, got, mid, ups, zb, err, rc, gws,
    pbx, pby, pbz, pbc,
    load_sem, gy, gx, gsend, sib_send, sib_recv, pr_sem,
    rx, ry, rz, rsend, ey, ex, es, esend, rc_sem, pen_recv, pen_send, out_sem,
):
    section, tensor = lax.axis_index("section"), lax.axis_index("tensor")
    z, c = section // 2, section % 2
    y, x = tensor // 4, tensor % 4
    h, k = x % 2, x // 2

    def dev(xx, yy, zz, co):
        return (zz * 2 + co, yy * 4 + xx)

    def at_x(i):
        return dev((x + i) % NX, y, z, c)

    def at_y(j):
        return dev(x, (y + j) % NY, z, c)

    def at_z(j):
        return dev(x, y, (z + j) % NZ, c)

    sib = dev(x, y, z, 1 - c)

    def push(src, dst, ssem, rsem, to):
        copy = pltpu.make_async_remote_copy(src, dst, ssem, rsem, device_id=to, device_id_type=MESH)
        copy.start()
        return copy

    def took(ref, ssem, rsem):
        return pltpu.make_async_remote_copy(ref, ref, ssem, rsem, device_id=sib, device_id_type=MESH)

    own = pltpu.make_async_copy(
        resid.at[:, pl.ds(pl.multiple_of(c * HALF, 128), HALF)], rg.at[x, y], load_sem.at[0])
    own.start()
    enc_load = pltpu.make_async_copy(
        wenc.at[:, pl.ds(pl.multiple_of(c * HALF, 128), HALF)], we.at[0], load_sem.at[1])
    enc_load.start()
    dec_load = [
        pltpu.make_async_copy(wdec.at[:, q * Q:(q + 1) * Q], wd.at[q], load_sem.at[2 + q]) for q in range(4)
    ]
    for copy in dec_load:
        copy.start()

    barrier = pltpu.get_barrier_semaphore()
    partners = [at_x(i) for i in (1, 2, 3)] + [at_y(j) for j in NEAR] + [at_z(j) for j in NEAR] + [sib]
    for p in partners:
        pl.semaphore_signal(barrier, 1, device_id=p, device_id_type=MESH)
    own.wait()
    pl.semaphore_wait(barrier, len(partners))

    for j in FAR:
        push(rg.at[x, y], rg.at[x, y], gsend.at[0], gy.at[y], at_y(j))
    for i in (2, 1, 3):
        push(rg.at[x, y], rg.at[x, y], gsend.at[1], gx.at[x], at_x(i))
    to_sib = [
        push(wenc.at[:, pl.ds(pl.multiple_of((1 - c) * HALF, 128), HALF)], we.at[1],
             sib_send.at[0], sib_recv.at[0], sib),
        push(benc, bs, sib_send.at[1], sib_recv.at[1], sib),
    ]
    for hh in range(2):
        to_sib.append(
            push(wdec.at[:, pl.ds(pl.multiple_of((2 * (1 - c) + hh) * Q, 128), Q)], wds.at[hh],
                 sib_send.at[2 + hh], sib_recv.at[2 + hh], sib))

    def pass_on(n, carry):
        yy = (y + near_step(n)) % NY
        took(rg.at[x, yy], gsend.at[0], gy.at[yy]).wait_recv()
        for i in (2, 1, 3):
            push(rg.at[x, yy], rg.at[x, yy], gsend.at[1], gx.at[x], at_x(i))
        return carry

    lax.fori_loop(0, 7, pass_on, 0)

    for copy in dec_load:
        copy.wait()
    norm2 = jnp.zeros((LAT, 1), F32)
    for q in range(4):
        w = wd[q].astype(F32)
        norm2 = norm2 + jnp.sum(w * w, axis=1, keepdims=True)
    norm_col = jnp.sqrt(norm2 + epsilon)
    norm_row = jnp.transpose(jnp.broadcast_to(norm_col, (LAT, 128)))[0:1, :]

    enc_load.wait()
    for i in (1, 3, 2):
        xx = (x + i) % NX
        took(rg.at[xx], gsend.at[1], gx.at[xx]).wait_recv()
    for kk in range(2):
        even, odd = rg[2 * kk].astype(F32), rg[2 * kk + 1].astype(F32)
        both = jnp.concatenate([even, odd], axis=1).reshape(64, HALF)
        lhs[kk * 64:(kk + 1) * 64, :] = both.astype(BF16)
    to_sib[0].wait_recv()
    to_sib[1].wait_recv()
    rows = lhs[...]
    contract = (((1,), (1,)), ((), ()))
    for o in range(2):
        px[o] = lax.dot_general(rows, we[o], contract, preferred_element_type=F32)
    pre_copy = push(px, pr, pr_sem.at[0], pr_sem.at[1], sib)
    pre_copy.wait_recv()
    cc[0] = jnp.maximum(px[0] + pr[1] + benc[...], 0.0).astype(BF16)
    cc[1] = jnp.maximum(px[1] + pr[0] + bs[...], 0.0).astype(BF16)

    for hh in range(2):
        to_sib[2 + hh].wait_recv()

    def decode(hq):
        total = jnp.dot(cc[0], wd[2 * c + hq], preferred_element_type=F32)
        total = total + jnp.dot(cc[1], wds[hq], preferred_element_type=F32)
        part[hq] = total.astype(BF16).reshape(2, NY, 8, Q)

    decode(1 - h)

    def scatter_odd(n, carry):
        yy = (y + far_step(n)) % NY
        for kk in range(2):
            xx = 2 * kk + 1 - h
            slot = (xx - x + NX) % NX - 1
            push(part.at[1 - h, kk, yy], got.at[yy, slot], rsend.at[0], rx.at[yy], dev(xx, y, z, c))
        return carry

    lax.fori_loop(0, NY, scatter_odd, 0)
    decode(h)

    def scatter_even(n, carry):
        yy = (y + far_step(n)) % NY
        push(part.at[h, 1 - k, yy], got.at[yy, 1], rsend.at[0], rx.at[yy], at_x(2))
        return carry

    lax.fori_loop(0, NY, scatter_even, 0)

    codes_f32 = cc[0].astype(F32)
    sums_row = jnp.sum(codes_f32, axis=0, keepdims=True)
    sums_col = jnp.transpose(jnp.broadcast_to(sums_row, (128, LAT)))[:, 0:1]
    pbx[x] = jnp.broadcast_to(jnp.sum(sums_row * norm_row), (8, 128))
    for i in (1, 2, 3):
        push(pbx.at[x], pbx.at[x], pen_send.at[0], pen_recv.at[0], at_x(i))

    def piece_sum(yy):
        total = part[h, k, yy].astype(F32)
        for i in range(3):
            total = total + got[yy, i].astype(F32)
        return total

    def scatter_y(n, carry):
        step = far_step(n)
        yy = (y + step) % NY
        took(got.at[yy], rsend.at[0], rx.at[yy]).wait_recv()
        mid[yy] = piece_sum(yy).astype(BF16)
        push(mid.at[yy], ups.at[step - 1], rsend.at[1], ry.at[0], at_y(step))
        return carry

    lax.fori_loop(0, 7, scatter_y, 0)
    took(pbx.at[pl.ds(0, 3)], pen_send.at[0], pen_recv.at[0]).wait_recv()
    pbx_sum = pbx[0] + pbx[1] + pbx[2] + pbx[3]
    pby[y] = pbx_sum
    for j in FAR:
        push(pby.at[y], pby.at[y], pen_send.at[1], pen_recv.at[1], at_y(j))
    took(got.at[y], rsend.at[0], rx.at[y]).wait_recv()
    acc = piece_sum(y)
    took(ups, rsend.at[1], ry.at[0]).wait_recv()
    for j in range(7):
        acc = acc + ups[j].astype(F32)
    zb[z] = acc.astype(BF16)
    for j in FAR:
        push(zb.at[z], zb.at[z], rsend.at[2], rz.at[0], at_z(j))

    cols = pl.ds(pl.multiple_of(h * Q, 128), Q)
    rows8 = jnp.concatenate([rg[2 * k, y, :, cols].astype(F32), rg[2 * k + 1, y, :, cols].astype(F32)], axis=0)
    bias = bdec[pl.ds(2 * c + h, 1), :]
    took(zb.at[pl.ds(0, 7)], rsend.at[2], rz.at[0]).wait_recv()
    total = zb[0].astype(F32)
    for j in range(1, NZ):
        total = total + zb[j].astype(F32)
    piece = total + bias
    err[c, x, y] = (piece - rows8).astype(BF16)
    rc[c, h] = piece
    for j in FAR:
        push(err.at[c, x, y], err.at[c, x, y], esend.at[0], ey.at[y], at_y(j))
    for i in (2, 1, 3):
        push(err.at[c, x, y], err.at[c, x, y], esend.at[1], ex.at[x], at_x(i))
    beside = dev(x + 1 - 2 * h, y, z, c)
    push(rc.at[c, h], rc.at[c, h], rc_sem.at[0], rc_sem.at[1], beside)
    took(pby.at[pl.ds(0, 7)], pen_send.at[1], pen_recv.at[1]).wait_recv()
    pen = pby[0]
    for j in range(1, NY):
        pen = pen + pby[j]
    pbz[z] = pen
    for j in FAR:
        push(pbz.at[z], pbz.at[z], pen_send.at[2], pen_recv.at[2], at_z(j))

    def pass_err(n, carry):
        yy = (y + near_step(n)) % NY
        took(err.at[c, x, yy], esend.at[0], ey.at[yy]).wait_recv()
        for i in (2, 1, 3):
            push(err.at[c, x, yy], err.at[c, x, yy], esend.at[1], ex.at[x], at_x(i))
        return carry

    lax.fori_loop(0, 7, pass_err, 0)
    push(err.at[c, x], err.at[c, x], esend.at[2], es.at[x], sib)
    took(rc.at[c, h], rc_sem.at[0], rc_sem.at[1]).wait_recv()
    push(rc.at[c], rc.at[c], rc_sem.at[2], rc_sem.at[3], sib)
    took(pbz.at[pl.ds(0, 7)], pen_send.at[2], pen_recv.at[2]).wait_recv()
    pen = pbz[0]
    for j in range(1, NZ):
        pen = pen + pbz[j]
    pbc[c] = pen
    push(pbc.at[c], pbc.at[c], pen_send.at[3], pen_recv.at[3], sib)
    for i in (2, 1, 3):
        xx = (x + i) % NX
        took(err.at[c, xx], esend.at[1], ex.at[xx]).wait_recv()
        push(err.at[c, xx], err.at[c, xx], esend.at[2], es.at[xx], sib)

    codes = cc[0]
    ratio = sums_col / norm_col

    def quarter(co, hq, cg):
        q = 2 * co + hq
        e = jnp.concatenate([err[co, hq].reshape(64, Q), err[co, 2 + hq].reshape(64, Q)], axis=0)
        w = wd[q]
        grad = lax.dot_general(codes, e, (((0,), (0,)), ((), ())), preferred_element_type=F32)
        gws[q] = (grad + ratio * w.astype(F32)).astype(BF16)
        pltpu.make_async_copy(
            gws.at[q], gw_o.at[:, pl.ds(pl.multiple_of(q * Q, 128), Q)], out_sem.at[q]).start()
        cg = cg + lax.dot_general(e, w, contract, preferred_element_type=F32)
        ef = e.astype(F32)
        gb_o[pl.ds(q, 1), :] = jnp.sum(ef, axis=0, keepdims=True)
        return cg, ef

    cg = jnp.zeros((ROWS, LAT), F32)
    cg, _ = quarter(c, h, cg)
    cg, _ = quarter(c, 1 - h, cg)
    for xx in range(4):
        took(err.at[1 - c, xx], esend.at[2], es.at[xx]).wait_recv()
    cg, _ = quarter(1 - c, 0, cg)
    cg, _ = quarter(1 - c, 1, cg)

    for kk in range(2):
        for yy in range(NY):
            at = kk * 64 + yy * 8
            cg_o[16 * yy + 8 * kk:16 * yy + 8 * kk + 8, :] = cg[at:at + 8] + norm_row

    squares = jnp.zeros((8, Q), F32)
    for co in range(2):
        for xx in range(NX):
            e = err[co, xx].astype(F32)
            squares = squares + jnp.sum(e * e, axis=0)
    took(pbc.at[c], pen_send.at[3], pen_recv.at[3]).wait_recv()
    loss_o[...] = (0.5 * jnp.sum(squares) + (pbc[0] + pbc[1])) * SCALE

    took(rc.at[c], rc_sem.at[2], rc_sem.at[3]).wait_recv()
    for co in range(2):
        for hq in range(2):
            q = 2 * co + hq
            v = rc[co, hq]
            recon_o[:, q * Q:(q + 1) * Q] = jnp.where(h == 0, v[0:4], v[4:8])

    took(rg.at[0, pl.ds(0, 7)], gsend.at[0], gy.at[0]).wait_send()
    took(rg.at[pl.ds(0, 3)], gsend.at[1], gx.at[0]).wait_send()
    for copy in to_sib:
        copy.wait_send()
    pre_copy.wait_send()
    took(got, rsend.at[0], rx.at[0]).wait_send()
    took(ups, rsend.at[1], ry.at[0]).wait_send()
    took(zb.at[pl.ds(0, 7)], rsend.at[2], rz.at[0]).wait_send()
    took(err.at[0, 0, pl.ds(0, 7)], esend.at[0], ey.at[0]).wait_send()
    took(err.at[0, pl.ds(0, 3)], esend.at[1], ex.at[0]).wait_send()
    took(err.at[0], esend.at[2], es.at[0]).wait_send()
    took(rc.at[0, 0], rc_sem.at[0], rc_sem.at[1]).wait_send()
    took(rc.at[0], rc_sem.at[2], rc_sem.at[3]).wait_send()
    took(pbx.at[pl.ds(0, 3)], pen_send.at[0], pen_recv.at[0]).wait_send()
    took(pby.at[pl.ds(0, 7)], pen_send.at[1], pen_recv.at[1]).wait_send()
    took(pbz.at[pl.ds(0, 7)], pen_send.at[2], pen_recv.at[2]).wait_send()
    took(pbc.at[0], pen_send.at[3], pen_recv.at[3]).wait_send()
    for q in range(4):
        pltpu.make_async_copy(gws.at[q], gw_o.at[:, q * Q:(q + 1) * Q], out_sem.at[q]).wait()


def per_device(resid, w_enc, b_enc, w_dec, b_dec):
    anywhere = pl.BlockSpec(memory_space=pl.ANY)
    vmem = pl.BlockSpec(memory_space=pltpu.VMEM)
    dma = pltpu.SemaphoreType.DMA
    recon, grad_w_dec, code_grad, grad_b_dec, loss = pl.pallas_call(
        kernel,
        out_shape=(
            jax.ShapeDtypeStruct((4, D), F32),
            jax.ShapeDtypeStruct((LAT, D), BF16),
            jax.ShapeDtypeStruct((ROWS, LAT), F32),
            jax.ShapeDtypeStruct((4, Q), F32),
            jax.ShapeDtypeStruct((8, 128), F32),
        ),
        in_specs=[anywhere, anywhere, vmem, anywhere, vmem],
        out_specs=(vmem, anywhere, vmem, vmem, vmem),
        scratch_shapes=[
            pltpu.VMEM((NX, NY, 4, HALF), BF16),
            pltpu.VMEM((2, LAT, HALF), BF16),
            pltpu.VMEM((4, LAT, Q), BF16),
            pltpu.VMEM((2, LAT, Q), BF16),
            pltpu.VMEM((1, LAT), F32),
            pltpu.VMEM((ROWS, HALF), BF16),
            pltpu.VMEM((2, ROWS, LAT), F32),
            pltpu.VMEM((2, ROWS, LAT), F32),
            pltpu.VMEM((2, ROWS, LAT), BF16),
            pltpu.VMEM((2, 2, NY, 8, Q), BF16),
            pltpu.VMEM((NY, 3, 8, Q), BF16),
            pltpu.VMEM((NY, 8, Q), BF16),
            pltpu.VMEM((7, 8, Q), BF16),
            pltpu.VMEM((NZ, 8, Q), BF16),
            pltpu.VMEM((2, NX, NY, 8, Q), BF16),
            pltpu.VMEM((2, 2, 8, Q), F32),
            pltpu.VMEM((4, LAT, Q), BF16),
            pltpu.VMEM((NX, 8, 128), F32),
            pltpu.VMEM((NY, 8, 128), F32),
            pltpu.VMEM((NZ, 8, 128), F32),
            pltpu.VMEM((2, 8, 128), F32),
            dma((6,)),
            dma((NY,)),
            dma((NX,)),
            dma((2,)),
            dma((4,)),
            dma((4,)),
            dma((2,)),
            dma((NY,)),
            dma((1,)),
            dma((1,)),
            dma((3,)),
            dma((NY,)),
            dma((NX,)),
            dma((NX,)),
            dma((3,)),
            dma((4,)),
            dma((4,)),
            dma((4,)),
            dma((4,)),
        ],
        compiler_params=pltpu.CompilerParams(
            collective_id=0, has_side_effects=True, vmem_limit_bytes=48 << 20
        ),
        cost_estimate=pl.CostEstimate(flops=900_000_000, bytes_accessed=6_000_000, transcendentals=0),
    )(resid, w_enc, b_enc.reshape(1, LAT), w_dec, b_dec.reshape(4, Q))
    return recon, grad_w_dec, code_grad, grad_b_dec.reshape(D), loss[0, 0]


def solution(mesh):
    in_specs = (
        P("tensor", None),
        P(("section", "tensor"), None),
        P(("section", "tensor")),
        P(("section", "tensor"), None),
        P(),
    )
    out_specs = (
        P("tensor", None),
        P(("section", "tensor"), None),
        P(None, ("section", "tensor")),
        P(),
        P(),
    )
    return jax.shard_map(
        per_device, mesh=mesh, in_specs=in_specs, out_specs=out_specs, check_vma=False
    )
```

```python
import functools

import jax
import jax.numpy as jnp
from jax import lax
from jax.experimental import pallas as pl
from jax.experimental.pallas import tpu as pltpu
from jax.sharding import PartitionSpec as P

MESH = pl.DeviceIdType.MESH
F32, BF16 = jnp.float32, jnp.bfloat16
epsilon = 1e-06

NX, NY, NZ = 4, 8, 8
D, LAT, ROWS = 3584, 224, 128
HALF, Q = D // 2, D // 4
SCALE = 1.0 / (ROWS * D)
NEAR = (1, 7, 2, 6, 3, 5, 4)
FAR = (4, 3, 5, 2, 6, 1, 7)


def far_step(n):
    return 4 + (1 - 2 * (n % 2)) * ((n + 1) // 2)


def near_step(n):
    return (1 - 2 * (n % 2)) * ((n + 2) // 2) + 8 * (n % 2)


def kernel(
    resid, wenc, benc, wdec, bdec,
    recon_o, gw_o, cg_o, gb_o, loss_o,
    rg, we, wd, wds, bo, bs, bd, lhs, px, pr, cc, part, got, mid, ups, zb, err, rc,
    pbx, pby, pbz, pbc,
    load_sem, gy, gx, gsend, sib_send, sib_recv, pr_sem,
    rx, ry, rz, rsend, ey, ex, es, esend, rc_sem, pen_recv, pen_send,
):
    section, tensor = lax.axis_index("section"), lax.axis_index("tensor")
    z, c = section // 2, section % 2
    y, x = tensor // 4, tensor % 4
    h, k = x % 2, x // 2

    def dev(xx, yy, zz, co):
        return (zz * 2 + co, yy * 4 + xx)

    def at_x(i):
        return dev((x + i) % NX, y, z, c)

    def at_y(j):
        return dev(x, (y + j) % NY, z, c)

    def at_z(j):
        return dev(x, y, (z + j) % NZ, c)

    sib = dev(x, y, z, 1 - c)

    def push(src, dst, ssem, rsem, to):
        copy = pltpu.make_async_remote_copy(src, dst, ssem, rsem, device_id=to, device_id_type=MESH)
        copy.start()
        return copy

    def took(ref, ssem, rsem):
        return pltpu.make_async_remote_copy(ref, ref, ssem, rsem, device_id=sib, device_id_type=MESH)

    sent = []

    own = pltpu.make_async_copy(
        resid.at[:, pl.ds(pl.multiple_of(c * HALF, 128), HALF)], rg.at[x, y], load_sem.at[0])
    own.start()
    enc_load = pltpu.make_async_copy(
        wenc.at[:, pl.ds(pl.multiple_of(c * HALF, 128), HALF)], we.at[0], load_sem.at[1])
    enc_load.start()
    dec_load = [
        pltpu.make_async_copy(wdec.at[:, q * Q:(q + 1) * Q], wd.at[q], load_sem.at[2 + q]) for q in range(4)
    ]
    for copy in dec_load:
        copy.start()
    bias_load = [
        pltpu.make_async_copy(benc, bo, load_sem.at[6]),
        pltpu.make_async_copy(bdec, bd, load_sem.at[7]),
    ]
    for copy in bias_load:
        copy.start()

    barrier = pltpu.get_barrier_semaphore()
    partners = [at_x(i) for i in (1, 2, 3)] + [at_y(j) for j in NEAR] + [at_z(j) for j in NEAR] + [sib]
    for p in partners:
        pl.semaphore_signal(barrier, 1, device_id=p, device_id_type=MESH)
    own.wait()
    pl.semaphore_wait(barrier, len(partners))

    for j in FAR:
        push(rg.at[x, y], rg.at[x, y], gsend.at[0], gy.at[y], at_y(j))
    for i in (2, 1, 3):
        push(rg.at[x, y], rg.at[x, y], gsend.at[1], gx.at[x], at_x(i))
    to_sib = [
        push(wenc.at[:, pl.ds(pl.multiple_of((1 - c) * HALF, 128), HALF)], we.at[1],
             sib_send.at[0], sib_recv.at[0], sib),
        push(benc, bs, sib_send.at[1], sib_recv.at[1], sib),
    ]
    for hh in range(2):
        to_sib.append(
            push(wdec.at[:, pl.ds(pl.multiple_of((2 * (1 - c) + hh) * Q, 128), Q)], wds.at[hh],
                 sib_send.at[2 + hh], sib_recv.at[2 + hh], sib))

    def pass_on(n, carry):
        yy = (y + near_step(n)) % NY
        took(rg.at[x, yy], gsend.at[0], gy.at[yy]).wait_recv()
        for i in (2, 1, 3):
            push(rg.at[x, yy], rg.at[x, yy], gsend.at[1], gx.at[x], at_x(i))
        return carry

    lax.fori_loop(0, 7, pass_on, 0)
    sent.append(took(rg.at[0, pl.ds(0, 7)], gsend.at[0], gy.at[0]))
    sent.append(took(rg.at[pl.ds(0, 3)], gsend.at[1], gx.at[0]))
    sent.extend(to_sib)

    for copy in dec_load:
        copy.wait()
    norm2 = jnp.zeros((LAT, 1), F32)
    for q in range(4):
        w = wd[q].astype(F32)
        norm2 = norm2 + jnp.sum(w * w, axis=1, keepdims=True)
    norm_col = jnp.sqrt(norm2 + epsilon)
    norm_row = jnp.transpose(jnp.broadcast_to(norm_col, (LAT, 128)))[0:1, :]

    enc_load.wait()
    for i in (1, 3, 2):
        xx = (x + i) % NX
        took(rg.at[xx], gsend.at[1], gx.at[xx]).wait_recv()
    for kk in range(2):
        even, odd = rg[2 * kk].astype(F32), rg[2 * kk + 1].astype(F32)
        lhs[:, kk] = jnp.concatenate([even, odd], axis=1).astype(BF16)
    to_sib[0].wait_recv()
    to_sib[1].wait_recv()
    rows = lhs[...].reshape(ROWS, HALF)
    for copy in bias_load:
        copy.wait()
    contract = (((1,), (1,)), ((), ()))
    for o in range(2):
        px[o] = lax.dot_general(rows, we[o], contract, preferred_element_type=F32)
    pre_copy = push(px, pr, pr_sem.at[0], pr_sem.at[1], sib)
    sent.append(pre_copy)
    pre_copy.wait_recv()
    cc[0] = jnp.maximum(px[0] + pr[1] + bo[...], 0.0).astype(BF16)
    cc[1] = jnp.maximum(px[1] + pr[0] + bs[...], 0.0).astype(BF16)

    for hh in range(2):
        to_sib[2 + hh].wait_recv()

    def decode(hq):
        total = jnp.dot(cc[0], wd[2 * c + hq], preferred_element_type=F32)
        total = total + jnp.dot(cc[1], wds[hq], preferred_element_type=F32)
        part[hq] = total.astype(BF16).reshape(NY, 2, 8, Q)

    decode(1 - h)

    def scatter_odd(n, carry):
        yy = (y + far_step(n)) % NY
        for kk in range(2):
            xx = 2 * kk + 1 - h
            slot = (xx - x + NX) % NX - 1
            push(part.at[1 - h, yy, kk], got.at[yy, slot], rsend.at[0], rx.at[yy], dev(xx, y, z, c))
        return carry

    lax.fori_loop(0, NY, scatter_odd, 0)
    decode(h)

    def scatter_even(n, carry):
        yy = (y + far_step(n)) % NY
        push(part.at[h, yy, 1 - k], got.at[yy, 1], rsend.at[0], rx.at[yy], at_x(2))
        return carry

    lax.fori_loop(0, NY, scatter_even, 0)
    sent.append(took(got, rsend.at[0], rx.at[0]))

    codes_f32 = cc[0].astype(F32)
    sums_row = jnp.sum(codes_f32, axis=0, keepdims=True)
    sums_col = jnp.transpose(jnp.broadcast_to(sums_row, (128, LAT)))[:, 0:1]
    pbx[x] = jnp.broadcast_to(jnp.sum(sums_row * norm_row), (8, 128))
    for i in (1, 2, 3):
        push(pbx.at[x], pbx.at[x], pen_send.at[0], pen_recv.at[0], at_x(i))
    sent.append(took(pbx.at[pl.ds(0, 3)], pen_send.at[0], pen_recv.at[0]))

    def piece_sum(yy):
        total = part[h, yy, k].astype(F32)
        for i in range(3):
            total = total + got[yy, i].astype(F32)
        return total

    def scatter_y(n, carry):
        step = far_step(n)
        yy = (y + step) % NY
        took(got.at[yy], rsend.at[0], rx.at[yy]).wait_recv()
        mid[yy] = piece_sum(yy).astype(BF16)
        push(mid.at[yy], ups.at[step - 1], rsend.at[1], ry.at[0], at_y(step))
        return carry

    lax.fori_loop(0, 7, scatter_y, 0)
    sent.append(took(ups, rsend.at[1], ry.at[0]))
    took(pbx.at[pl.ds(0, 3)], pen_send.at[0], pen_recv.at[0]).wait_recv()
    pbx_sum = pbx[0] + pbx[1] + pbx[2] + pbx[3]
    pby[y] = pbx_sum
    for j in FAR:
        push(pby.at[y], pby.at[y], pen_send.at[1], pen_recv.at[1], at_y(j))
    sent.append(took(pby.at[pl.ds(0, 7)], pen_send.at[1], pen_recv.at[1]))
    took(got.at[y], rsend.at[0], rx.at[y]).wait_recv()
    acc = piece_sum(y)
    took(ups, rsend.at[1], ry.at[0]).wait_recv()
    for j in range(7):
        acc = acc + ups[j].astype(F32)
    zb[z] = acc.astype(BF16)
    for j in FAR:
        push(zb.at[z], zb.at[z], rsend.at[2], rz.at[0], at_z(j))
    sent.append(took(zb.at[pl.ds(0, 7)], rsend.at[2], rz.at[0]))

    cols = pl.ds(pl.multiple_of(h * Q, 128), Q)
    rows8 = jnp.concatenate([rg[2 * k, y, :, cols].astype(F32), rg[2 * k + 1, y, :, cols].astype(F32)], axis=0)
    first = (2 * c + h) * 7
    bias = jnp.concatenate([bd[pl.ds(first + i, 1), :] for i in range(7)], axis=1)
    took(zb.at[pl.ds(0, 7)], rsend.at[2], rz.at[0]).wait_recv()
    total = zb[0].astype(F32)
    for j in range(1, NZ):
        total = total + zb[j].astype(F32)
    piece = total + bias
    err[c, x, y] = (piece - rows8).astype(BF16)
    rc[c, h] = piece
    for j in FAR:
        push(err.at[c, x, y], err.at[c, x, y], esend.at[0], ey.at[y], at_y(j))
    for i in (2, 1, 3):
        push(err.at[c, x, y], err.at[c, x, y], esend.at[1], ex.at[x], at_x(i))
    beside = dev(x + 1 - 2 * h, y, z, c)
    push(rc.at[c, h], rc.at[c, h], rc_sem.at[0], rc_sem.at[1], beside)
    sent.append(took(rc.at[0, 0], rc_sem.at[0], rc_sem.at[1]))
    took(pby.at[pl.ds(0, 7)], pen_send.at[1], pen_recv.at[1]).wait_recv()
    pen = pby[0]
    for j in range(1, NY):
        pen = pen + pby[j]
    pbz[z] = pen
    for j in FAR:
        push(pbz.at[z], pbz.at[z], pen_send.at[2], pen_recv.at[2], at_z(j))
    sent.append(took(pbz.at[pl.ds(0, 7)], pen_send.at[2], pen_recv.at[2]))

    def pass_err(n, carry):
        yy = (y + near_step(n)) % NY
        took(err.at[c, x, yy], esend.at[0], ey.at[yy]).wait_recv()
        for i in (2, 1, 3):
            push(err.at[c, x, yy], err.at[c, x, yy], esend.at[1], ex.at[x], at_x(i))
        return carry

    lax.fori_loop(0, 7, pass_err, 0)
    sent.append(took(err.at[0, 0, pl.ds(0, 7)], esend.at[0], ey.at[0]))
    sent.append(took(err.at[0, pl.ds(0, 3)], esend.at[1], ex.at[0]))
    push(err.at[c, x], err.at[c, x], esend.at[2], es.at[x], sib)
    took(rc.at[c, h], rc_sem.at[0], rc_sem.at[1]).wait_recv()
    push(rc.at[c], rc.at[c], rc_sem.at[2], rc_sem.at[3], sib)
    sent.append(took(rc.at[0], rc_sem.at[2], rc_sem.at[3]))
    took(pbz.at[pl.ds(0, 7)], pen_send.at[2], pen_recv.at[2]).wait_recv()
    pen = pbz[0]
    for j in range(1, NZ):
        pen = pen + pbz[j]
    pbc[c] = pen
    push(pbc.at[c], pbc.at[c], pen_send.at[3], pen_recv.at[3], sib)
    sent.append(took(pbc.at[0], pen_send.at[3], pen_recv.at[3]))
    for i in (2, 1, 3):
        xx = (x + i) % NX
        took(err.at[c, xx], esend.at[1], ex.at[xx]).wait_recv()
        push(err.at[c, xx], err.at[c, xx], esend.at[2], es.at[xx], sib)
    sent.append(took(err.at[0], esend.at[2], es.at[0]))

    codes = cc[0]
    ratio = sums_col / norm_col

    def quarter(co, hq, cg):
        q = 2 * co + hq
        e = jnp.stack([err[co, hq], err[co, 2 + hq]], axis=1).reshape(ROWS, Q)
        w = wd[q]
        grad = lax.dot_general(codes, e, (((0,), (0,)), ((), ())), preferred_element_type=F32)
        gw_o[q] = (grad + ratio * w.astype(F32)).astype(BF16)
        sums = jnp.sum(e.astype(F32), axis=0, keepdims=True)
        for i in range(7):
            gb_o[pl.ds(7 * q + i, 1), :] = sums[:, i * 128:(i + 1) * 128]
        return cg + lax.dot_general(w, e, contract, preferred_element_type=F32)

    cg = jnp.zeros((LAT, ROWS), F32)
    cg = quarter(c, h, cg)
    cg = quarter(c, 1 - h, cg)
    for xx in range(4):
        took(err.at[1 - c, xx], esend.at[2], es.at[xx]).wait_recv()
    cg = quarter(1 - c, 0, cg)
    cg = quarter(1 - c, 1, cg)
    cg_o[...] = cg + norm_col

    squares = jnp.zeros((8, Q), F32)
    for co in range(2):
        for xx in range(NX):
            e = err[co, xx].astype(F32)
            squares = squares + jnp.sum(e * e, axis=0)
    took(pbc.at[c], pen_send.at[3], pen_recv.at[3]).wait_recv()
    loss_o[...] = (0.5 * jnp.sum(squares) + (pbc[0] + pbc[1])) * SCALE

    took(rc.at[c], rc_sem.at[2], rc_sem.at[3]).wait_recv()
    for co in range(2):
        for hq in range(2):
            q = 2 * co + hq
            v = rc[co, hq]
            recon_o[:, q * Q:(q + 1) * Q] = jnp.where(h == 0, v[0:4], v[4:8])

    for copy in sent:
        copy.wait_send()


def write_out(recon, grad, code_grad, bias_grad, loss, recon_o, grad_o, code_grad_o, bias_grad_o, loss_o, sem):
    copies = [pltpu.make_async_copy(grad.at[q], grad_o.at[:, q * Q:(q + 1) * Q], sem.at[q]) for q in range(4)]
    copies += [
        pltpu.make_async_copy(recon, recon_o, sem.at[4]),
        pltpu.make_async_copy(code_grad, code_grad_o, sem.at[5]),
        pltpu.make_async_copy(bias_grad, bias_grad_o, sem.at[6]),
    ]
    for copy in copies:
        copy.start()
    loss_o[...] = loss[0:1, 0:1]
    for copy in copies:
        copy.wait()


def per_device(resid, w_enc, b_enc, w_dec, b_dec):
    hbm = pl.BlockSpec(memory_space=pltpu.HBM)
    vmem = pl.BlockSpec(memory_space=pltpu.VMEM)
    dma = pltpu.SemaphoreType.DMA
    made = pl.pallas_call(
        kernel,
        out_shape=(
            jax.ShapeDtypeStruct((4, D), F32),
            jax.ShapeDtypeStruct((4, LAT, Q), BF16),
            jax.ShapeDtypeStruct((LAT, ROWS), F32),
            jax.ShapeDtypeStruct((28, 128), F32),
            jax.ShapeDtypeStruct((8, 128), F32),
        ),
        in_specs=[hbm] * 5,
        out_specs=(vmem,) * 5,
        scratch_shapes=[
            pltpu.VMEM((NX, NY, 4, HALF), BF16),
            pltpu.VMEM((2, LAT, HALF), BF16),
            pltpu.VMEM((4, LAT, Q), BF16),
            pltpu.VMEM((2, LAT, Q), BF16),
            pltpu.VMEM((1, LAT), F32),
            pltpu.VMEM((1, LAT), F32),
            pltpu.VMEM((28, 128), F32),
            pltpu.VMEM((NY, 2, 8, HALF), BF16),
            pltpu.VMEM((2, ROWS, LAT), F32),
            pltpu.VMEM((2, ROWS, LAT), F32),
            pltpu.VMEM((2, ROWS, LAT), BF16),
            pltpu.VMEM((2, NY, 2, 8, Q), BF16),
            pltpu.VMEM((NY, 3, 8, Q), BF16),
            pltpu.VMEM((NY, 8, Q), BF16),
            pltpu.VMEM((7, 8, Q), BF16),
            pltpu.VMEM((NZ, 8, Q), BF16),
            pltpu.VMEM((2, NX, NY, 8, Q), BF16),
            pltpu.VMEM((2, 2, 8, Q), F32),
            pltpu.VMEM((NX, 8, 128), F32),
            pltpu.VMEM((NY, 8, 128), F32),
            pltpu.VMEM((NZ, 8, 128), F32),
            pltpu.VMEM((2, 8, 128), F32),
            dma((8,)),
            dma((NY,)),
            dma((NX,)),
            dma((2,)),
            dma((4,)),
            dma((4,)),
            dma((2,)),
            dma((NY,)),
            dma((1,)),
            dma((1,)),
            dma((3,)),
            dma((NY,)),
            dma((NX,)),
            dma((NX,)),
            dma((3,)),
            dma((4,)),
            dma((4,)),
            dma((4,)),
        ],
        compiler_params=pltpu.CompilerParams(
            collective_id=0, has_side_effects=True, vmem_limit_bytes=48 << 20
        ),
        cost_estimate=pl.CostEstimate(flops=900_000_000, bytes_accessed=6_000_000, transcendentals=0),
    )(*[pltpu.with_memory_space_constraint(v, pltpu.HBM) for v in (resid, w_enc, b_enc.reshape(1, LAT), w_dec, b_dec.reshape(28, 128))])
    recon, grad_w_dec, code_grad, grad_b_dec, loss = pl.pallas_call(
        write_out,
        out_shape=(
            jax.ShapeDtypeStruct((4, D), F32),
            jax.ShapeDtypeStruct((LAT, D), BF16),
            jax.ShapeDtypeStruct((LAT, ROWS), F32),
            jax.ShapeDtypeStruct((28, 128), F32),
            jax.ShapeDtypeStruct((1, 1), F32),
        ),
        in_specs=[vmem] * 5,
        out_specs=(hbm,) * 4 + (vmem,),
        scratch_shapes=[dma((7,))],
        compiler_params=pltpu.CompilerParams(vmem_limit_bytes=1 << 20),
    )(*made)
    return recon, grad_w_dec, code_grad.T, grad_b_dec.reshape(D), loss.reshape(())


def solution(mesh):
    in_specs = (
        P("tensor", None),
        P(("section", "tensor"), None),
        P(("section", "tensor")),
        P(("section", "tensor"), None),
        P(),
    )
    out_specs = (
        P("tensor", None),
        P(("section", "tensor"), None),
        P(None, ("section", "tensor")),
        P(),
        P(),
    )
    return jax.shard_map(
        per_device, mesh=mesh, in_specs=in_specs, out_specs=out_specs, check_vma=False
    )
```

```python
import functools

import jax
import jax.numpy as jnp
from jax import lax
from jax.experimental import pallas as pl
from jax.experimental.pallas import tpu as pltpu
from jax.sharding import PartitionSpec as P

MESH = pl.DeviceIdType.MESH
F32, BF16 = jnp.float32, jnp.bfloat16
epsilon = 1e-06

NX, NY, NZ = 4, 8, 8
D, LAT, ROWS = 3584, 224, 128
HALF, Q = D // 2, D // 4
SCALE = 1.0 / (ROWS * D)
NEAR = (1, 7, 2, 6, 3, 5, 4)
FAR = (4, 3, 5, 2, 6, 1, 7)


def far_step(n):
    return 4 + (1 - 2 * (n % 2)) * ((n + 1) // 2)


def near_step(n):
    return (1 - 2 * (n % 2)) * ((n + 2) // 2) + 8 * (n % 2)


def kernel(
    resid, wenc, benc, wdec, bdec,
    recon_o, gw_o, cg_o, gb_o, loss_o,
    rg, we, wd, wds, bo, bs, bd, lhs, px, pr, cc, part, got, mid, ups, zb, err, rc,
    pbx, pby, pbz, pbc,
    load_sem, gy, gx, gsend, sib_send, sib_recv, pr_sem,
    rx, ry, rz, rsend, ey, ex, es, esend, rc_sem, pen_recv, pen_send,
):
    section, tensor = lax.axis_index("section"), lax.axis_index("tensor")
    z, c = section // 2, section % 2
    y, x = tensor // 4, tensor % 4
    h, k = x % 2, x // 2

    def dev(xx, yy, zz, co):
        return (zz * 2 + co, yy * 4 + xx)

    def at_x(i):
        return dev((x + i) % NX, y, z, c)

    def at_y(j):
        return dev(x, (y + j) % NY, z, c)

    def at_z(j):
        return dev(x, y, (z + j) % NZ, c)

    sib = dev(x, y, z, 1 - c)

    def push(src, dst, ssem, rsem, to):
        copy = pltpu.make_async_remote_copy(src, dst, ssem, rsem, device_id=to, device_id_type=MESH)
        copy.start()
        return copy

    def took(ref, ssem, rsem):
        return pltpu.make_async_remote_copy(ref, ref, ssem, rsem, device_id=sib, device_id_type=MESH)

    sent = []

    own = pltpu.make_async_copy(
        resid.at[:, pl.ds(pl.multiple_of(c * HALF, 128), HALF)], rg.at[x, y], load_sem.at[0])
    own.start()
    enc_load = pltpu.make_async_copy(
        wenc.at[:, pl.ds(pl.multiple_of(c * HALF, 128), HALF)], we.at[0], load_sem.at[1])
    enc_load.start()
    dec_load = [
        pltpu.make_async_copy(wdec.at[:, q * Q:(q + 1) * Q], wd.at[q], load_sem.at[2 + q]) for q in range(4)
    ]
    for copy in dec_load:
        copy.start()
    bias_load = [
        pltpu.make_async_copy(benc, bo, load_sem.at[6]),
        pltpu.make_async_copy(bdec, bd, load_sem.at[7]),
    ]
    for copy in bias_load:
        copy.start()

    barrier = pltpu.get_barrier_semaphore()
    partners = [at_x(i) for i in (1, 2, 3)] + [at_y(j) for j in NEAR] + [at_z(j) for j in NEAR] + [sib]
    for p in partners:
        pl.semaphore_signal(barrier, 1, device_id=p, device_id_type=MESH)
    own.wait()
    pl.semaphore_wait(barrier, len(partners))

    for j in NEAR:
        push(rg.at[x, y], rg.at[x, y], gsend.at[0], gy.at[y], at_y(j))
    for i in (2, 1, 3):
        push(rg.at[x, y], rg.at[x, y], gsend.at[1], gx.at[x], at_x(i))
    def pass_on(n, carry):
        yy = (y + near_step(n)) % NY
        took(rg.at[x, yy], gsend.at[0], gy.at[yy]).wait_recv()
        for i in (2, 1, 3):
            push(rg.at[x, yy], rg.at[x, yy], gsend.at[1], gx.at[x], at_x(i))
        return carry

    lax.fori_loop(0, 7, pass_on, 0)
    to_sib = [
        push(wenc.at[:, pl.ds(pl.multiple_of((1 - c) * HALF, 128), HALF)], we.at[1],
             sib_send.at[0], sib_recv.at[0], sib),
        push(benc, bs, sib_send.at[1], sib_recv.at[1], sib),
    ]
    for hh in range(2):
        to_sib.append(
            push(wdec.at[:, pl.ds(pl.multiple_of((2 * (1 - c) + hh) * Q, 128), Q)], wds.at[hh],
                 sib_send.at[2 + hh], sib_recv.at[2 + hh], sib))
    sent.append(took(rg.at[0, pl.ds(0, 7)], gsend.at[0], gy.at[0]))
    sent.append(took(rg.at[pl.ds(0, 3)], gsend.at[1], gx.at[0]))
    sent.extend(to_sib)

    for copy in dec_load:
        copy.wait()
    norm2 = jnp.zeros((LAT, 1), F32)
    for q in range(4):
        w = wd[q].astype(F32)
        norm2 = norm2 + jnp.sum(w * w, axis=1, keepdims=True)
    norm_col = jnp.sqrt(norm2 + epsilon)
    norm_row = jnp.transpose(jnp.broadcast_to(norm_col, (LAT, 128)))[0:1, :]

    enc_load.wait()
    for i in (1, 3, 2):
        xx = (x + i) % NX
        took(rg.at[xx], gsend.at[1], gx.at[xx]).wait_recv()
    for kk in range(2):
        even, odd = rg[2 * kk].astype(F32), rg[2 * kk + 1].astype(F32)
        lhs[:, kk] = jnp.concatenate([even, odd], axis=1).astype(BF16)
    to_sib[0].wait_recv()
    to_sib[1].wait_recv()
    rows = lhs[...].reshape(ROWS, HALF)
    for copy in bias_load:
        copy.wait()
    contract = (((1,), (1,)), ((), ()))
    for o in range(2):
        px[o] = lax.dot_general(rows, we[o], contract, preferred_element_type=F32)
    pre_copy = push(px, pr, pr_sem.at[0], pr_sem.at[1], sib)
    sent.append(pre_copy)
    pre_copy.wait_recv()
    cc[0] = jnp.maximum(px[0] + pr[1] + bo[...], 0.0).astype(BF16)
    cc[1] = jnp.maximum(px[1] + pr[0] + bs[...], 0.0).astype(BF16)

    for hh in range(2):
        to_sib[2 + hh].wait_recv()

    def decode(hq):
        total = jnp.dot(cc[0], wd[2 * c + hq], preferred_element_type=F32)
        total = total + jnp.dot(cc[1], wds[hq], preferred_element_type=F32)
        part[hq] = total.astype(BF16).reshape(NY, 2, 8, Q)

    decode(1 - h)

    def scatter_odd(n, carry):
        yy = (y + far_step(n)) % NY
        for kk in range(2):
            xx = 2 * kk + 1 - h
            slot = (xx - x + NX) % NX - 1
            push(part.at[1 - h, yy, kk], got.at[yy, slot], rsend.at[0], rx.at[yy], dev(xx, y, z, c))
        return carry

    lax.fori_loop(0, NY, scatter_odd, 0)
    decode(h)

    def scatter_even(n, carry):
        yy = (y + far_step(n)) % NY
        push(part.at[h, yy, 1 - k], got.at[yy, 1], rsend.at[0], rx.at[yy], at_x(2))
        return carry

    lax.fori_loop(0, NY, scatter_even, 0)
    sent.append(took(got, rsend.at[0], rx.at[0]))

    codes_f32 = cc[0].astype(F32)
    sums_row = jnp.sum(codes_f32, axis=0, keepdims=True)
    sums_col = jnp.transpose(jnp.broadcast_to(sums_row, (128, LAT)))[:, 0:1]
    pbx[x] = jnp.broadcast_to(jnp.sum(sums_row * norm_row), (8, 128))
    for i in (1, 2, 3):
        push(pbx.at[x], pbx.at[x], pen_send.at[0], pen_recv.at[0], at_x(i))
    sent.append(took(pbx.at[pl.ds(0, 3)], pen_send.at[0], pen_recv.at[0]))

    def piece_sum(yy):
        total = part[h, yy, k].astype(F32)
        for i in range(3):
            total = total + got[yy, i].astype(F32)
        return total

    def scatter_y(n, carry):
        step = far_step(n)
        yy = (y + step) % NY
        took(got.at[yy], rsend.at[0], rx.at[yy]).wait_recv()
        mid[yy] = piece_sum(yy).astype(BF16)
        push(mid.at[yy], ups.at[step - 1], rsend.at[1], ry.at[0], at_y(step))
        return carry

    lax.fori_loop(0, 7, scatter_y, 0)
    sent.append(took(ups, rsend.at[1], ry.at[0]))
    took(pbx.at[pl.ds(0, 3)], pen_send.at[0], pen_recv.at[0]).wait_recv()
    pbx_sum = pbx[0] + pbx[1] + pbx[2] + pbx[3]
    pby[y] = pbx_sum
    for j in FAR:
        push(pby.at[y], pby.at[y], pen_send.at[1], pen_recv.at[1], at_y(j))
    sent.append(took(pby.at[pl.ds(0, 7)], pen_send.at[1], pen_recv.at[1]))
    took(got.at[y], rsend.at[0], rx.at[y]).wait_recv()
    acc = piece_sum(y)
    took(ups, rsend.at[1], ry.at[0]).wait_recv()
    for j in range(7):
        acc = acc + ups[j].astype(F32)
    zb[z] = acc.astype(BF16)
    for j in FAR:
        push(zb.at[z], zb.at[z], rsend.at[2], rz.at[0], at_z(j))
    sent.append(took(zb.at[pl.ds(0, 7)], rsend.at[2], rz.at[0]))

    cols = pl.ds(pl.multiple_of(h * Q, 128), Q)
    rows8 = jnp.concatenate([rg[2 * k, y, :, cols].astype(F32), rg[2 * k + 1, y, :, cols].astype(F32)], axis=0)
    first = (2 * c + h) * 7
    bias = jnp.concatenate([bd[pl.ds(first + i, 1), :] for i in range(7)], axis=1)
    took(zb.at[pl.ds(0, 7)], rsend.at[2], rz.at[0]).wait_recv()
    total = zb[0].astype(F32)
    for j in range(1, NZ):
        total = total + zb[j].astype(F32)
    piece = total + bias
    err[c, x, y] = (piece - rows8).astype(BF16)
    rc[c, h] = piece
    for j in NEAR:
        push(err.at[c, x, y], err.at[c, x, y], esend.at[0], ey.at[y], at_y(j))
    for i in (2, 1, 3):
        push(err.at[c, x, y], err.at[c, x, y], esend.at[1], ex.at[x], at_x(i))
    beside = dev(x + 1 - 2 * h, y, z, c)
    push(rc.at[c, h], rc.at[c, h], rc_sem.at[0], rc_sem.at[1], beside)
    sent.append(took(rc.at[0, 0], rc_sem.at[0], rc_sem.at[1]))
    took(pby.at[pl.ds(0, 7)], pen_send.at[1], pen_recv.at[1]).wait_recv()
    pen = pby[0]
    for j in range(1, NY):
        pen = pen + pby[j]
    pbz[z] = pen
    for j in FAR:
        push(pbz.at[z], pbz.at[z], pen_send.at[2], pen_recv.at[2], at_z(j))
    sent.append(took(pbz.at[pl.ds(0, 7)], pen_send.at[2], pen_recv.at[2]))

    def pass_err(n, carry):
        yy = (y + near_step(n)) % NY
        took(err.at[c, x, yy], esend.at[0], ey.at[yy]).wait_recv()
        for i in (2, 1, 3):
            push(err.at[c, x, yy], err.at[c, x, yy], esend.at[1], ex.at[x], at_x(i))
        return carry

    lax.fori_loop(0, 7, pass_err, 0)
    sent.append(took(err.at[0, 0, pl.ds(0, 7)], esend.at[0], ey.at[0]))
    sent.append(took(err.at[0, pl.ds(0, 3)], esend.at[1], ex.at[0]))
    push(err.at[c, x], err.at[c, x], esend.at[2], es.at[x], sib)
    took(rc.at[c, h], rc_sem.at[0], rc_sem.at[1]).wait_recv()
    push(rc.at[c], rc.at[c], rc_sem.at[2], rc_sem.at[3], sib)
    sent.append(took(rc.at[0], rc_sem.at[2], rc_sem.at[3]))
    took(pbz.at[pl.ds(0, 7)], pen_send.at[2], pen_recv.at[2]).wait_recv()
    pen = pbz[0]
    for j in range(1, NZ):
        pen = pen + pbz[j]
    pbc[c] = pen
    push(pbc.at[c], pbc.at[c], pen_send.at[3], pen_recv.at[3], sib)
    sent.append(took(pbc.at[0], pen_send.at[3], pen_recv.at[3]))
    for i in (2, 1, 3):
        xx = (x + i) % NX
        took(err.at[c, xx], esend.at[1], ex.at[xx]).wait_recv()
        push(err.at[c, xx], err.at[c, xx], esend.at[2], es.at[xx], sib)
    sent.append(took(err.at[0], esend.at[2], es.at[0]))

    codes = cc[0]
    ratio = sums_col / norm_col

    def quarter(co, hq, cg):
        q = 2 * co + hq
        e = jnp.stack([err[co, hq], err[co, 2 + hq]], axis=1).reshape(ROWS, Q)
        w = wd[q]
        grad = lax.dot_general(codes, e, (((0,), (0,)), ((), ())), preferred_element_type=F32)
        gw_o[q] = (grad + ratio * w.astype(F32)).astype(BF16)
        sums = jnp.sum(e.astype(F32), axis=0, keepdims=True)
        for i in range(7):
            gb_o[pl.ds(7 * q + i, 1), :] = sums[:, i * 128:(i + 1) * 128]
        return cg + lax.dot_general(w, e, contract, preferred_element_type=F32)

    cg = jnp.zeros((LAT, ROWS), F32)
    cg = quarter(c, h, cg)
    cg = quarter(c, 1 - h, cg)
    for xx in range(4):
        took(err.at[1 - c, xx], esend.at[2], es.at[xx]).wait_recv()
    cg = quarter(1 - c, 0, cg)
    cg = quarter(1 - c, 1, cg)
    cg_o[...] = cg + norm_col

    squares = jnp.zeros((8, Q), F32)
    for co in range(2):
        for xx in range(NX):
            e = err[co, xx].astype(F32)
            squares = squares + jnp.sum(e * e, axis=0)
    took(pbc.at[c], pen_send.at[3], pen_recv.at[3]).wait_recv()
    loss_o[...] = (0.5 * jnp.sum(squares) + (pbc[0] + pbc[1])) * SCALE

    took(rc.at[c], rc_sem.at[2], rc_sem.at[3]).wait_recv()
    for co in range(2):
        for hq in range(2):
            q = 2 * co + hq
            v = rc[co, hq]
            recon_o[:, q * Q:(q + 1) * Q] = jnp.where(h == 0, v[0:4], v[4:8])

    for copy in sent:
        copy.wait_send()


def write_out(recon, grad, code_grad, bias_grad, loss, recon_o, grad_o, code_grad_o, bias_grad_o, loss_o, sem):
    copies = [pltpu.make_async_copy(grad.at[q], grad_o.at[:, q * Q:(q + 1) * Q], sem.at[q]) for q in range(4)]
    copies += [
        pltpu.make_async_copy(recon, recon_o, sem.at[4]),
        pltpu.make_async_copy(code_grad, code_grad_o, sem.at[5]),
        pltpu.make_async_copy(bias_grad, bias_grad_o, sem.at[6]),
    ]
    for copy in copies:
        copy.start()
    loss_o[...] = loss[0:1, 0:1]
    for copy in copies:
        copy.wait()


def per_device(resid, w_enc, b_enc, w_dec, b_dec):
    hbm = pl.BlockSpec(memory_space=pltpu.HBM)
    vmem = pl.BlockSpec(memory_space=pltpu.VMEM)
    dma = pltpu.SemaphoreType.DMA
    made = pl.pallas_call(
        kernel,
        out_shape=(
            jax.ShapeDtypeStruct((4, D), F32),
            jax.ShapeDtypeStruct((4, LAT, Q), BF16),
            jax.ShapeDtypeStruct((LAT, ROWS), F32),
            jax.ShapeDtypeStruct((28, 128), F32),
            jax.ShapeDtypeStruct((8, 128), F32),
        ),
        in_specs=[hbm] * 5,
        out_specs=(vmem,) * 5,
        scratch_shapes=[
            pltpu.VMEM((NX, NY, 4, HALF), BF16),
            pltpu.VMEM((2, LAT, HALF), BF16),
            pltpu.VMEM((4, LAT, Q), BF16),
            pltpu.VMEM((2, LAT, Q), BF16),
            pltpu.VMEM((1, LAT), F32),
            pltpu.VMEM((1, LAT), F32),
            pltpu.VMEM((28, 128), F32),
            pltpu.VMEM((NY, 2, 8, HALF), BF16),
            pltpu.VMEM((2, ROWS, LAT), F32),
            pltpu.VMEM((2, ROWS, LAT), F32),
            pltpu.VMEM((2, ROWS, LAT), BF16),
            pltpu.VMEM((2, NY, 2, 8, Q), BF16),
            pltpu.VMEM((NY, 3, 8, Q), BF16),
            pltpu.VMEM((NY, 8, Q), BF16),
            pltpu.VMEM((7, 8, Q), BF16),
            pltpu.VMEM((NZ, 8, Q), BF16),
            pltpu.VMEM((2, NX, NY, 8, Q), BF16),
            pltpu.VMEM((2, 2, 8, Q), F32),
            pltpu.VMEM((NX, 8, 128), F32),
            pltpu.VMEM((NY, 8, 128), F32),
            pltpu.VMEM((NZ, 8, 128), F32),
            pltpu.VMEM((2, 8, 128), F32),
            dma((8,)),
            dma((NY,)),
            dma((NX,)),
            dma((2,)),
            dma((4,)),
            dma((4,)),
            dma((2,)),
            dma((NY,)),
            dma((1,)),
            dma((1,)),
            dma((3,)),
            dma((NY,)),
            dma((NX,)),
            dma((NX,)),
            dma((3,)),
            dma((4,)),
            dma((4,)),
            dma((4,)),
        ],
        compiler_params=pltpu.CompilerParams(
            collective_id=0, has_side_effects=True, vmem_limit_bytes=48 << 20
        ),
        cost_estimate=pl.CostEstimate(flops=900_000_000, bytes_accessed=6_000_000, transcendentals=0),
    )(*[pltpu.with_memory_space_constraint(v, pltpu.HBM) for v in (resid, w_enc, b_enc.reshape(1, LAT), w_dec, b_dec.reshape(28, 128))])
    recon, grad_w_dec, code_grad, grad_b_dec, loss = pl.pallas_call(
        write_out,
        out_shape=(
            jax.ShapeDtypeStruct((4, D), F32),
            jax.ShapeDtypeStruct((LAT, D), BF16),
            jax.ShapeDtypeStruct((LAT, ROWS), F32),
            jax.ShapeDtypeStruct((28, 128), F32),
            jax.ShapeDtypeStruct((1, 1), F32),
        ),
        in_specs=[vmem] * 5,
        out_specs=(hbm,) * 4 + (vmem,),
        scratch_shapes=[dma((7,))],
        compiler_params=pltpu.CompilerParams(vmem_limit_bytes=1 << 20),
    )(*made)
    return recon, grad_w_dec, code_grad.T, grad_b_dec.reshape(D), loss.reshape(())


def solution(mesh):
    in_specs = (
        P("tensor", None),
        P(("section", "tensor"), None),
        P(("section", "tensor")),
        P(("section", "tensor"), None),
        P(),
    )
    out_specs = (
        P("tensor", None),
        P(("section", "tensor"), None),
        P(None, ("section", "tensor")),
        P(),
        P(),
    )
    return jax.shard_map(
        per_device, mesh=mesh, in_specs=in_specs, out_specs=out_specs, check_vma=False
    )
```

```python
import functools

import jax
import jax.numpy as jnp
from jax import lax
from jax.experimental import pallas as pl
from jax.experimental.pallas import tpu as pltpu
from jax.sharding import PartitionSpec as P

MESH = pl.DeviceIdType.MESH
F32, BF16 = jnp.float32, jnp.bfloat16
epsilon = 1e-06

NX, NY, NZ = 4, 8, 8
D, LAT, ROWS = 3584, 224, 128
HALF, Q = D // 2, D // 4
SCALE = 1.0 / (ROWS * D)
NEAR = (1, 7, 2, 6, 3, 5, 4)
FAR = (4, 3, 5, 2, 6, 1, 7)


def far_step(n):
    return 4 + (1 - 2 * (n % 2)) * ((n + 1) // 2)


def near_step(n):
    return (1 - 2 * (n % 2)) * ((n + 2) // 2) + 8 * (n % 2)


def kernel(
    resid, wenc, benc, wdec, bdec,
    recon_o, gw_o, cg_o, gb_o, loss_o,
    rg, we, wd, wds, bo, bs, bd, lhs, px, pr, cc, part, got, mid, ups, zb, err, rc,
    pbx, pby, pbz, pbc,
    load_sem, gy, gx, gsend, sib_send, sib_recv, pr_sem,
    rx, ry, rz, rsend, ey, ex, es, esend, rc_sem, pen_recv, pen_send,
):
    section, tensor = lax.axis_index("section"), lax.axis_index("tensor")
    z, c = section // 2, section % 2
    y, x = tensor // 4, tensor % 4
    h, k = x % 2, x // 2

    def dev(xx, yy, zz, co):
        return (zz * 2 + co, yy * 4 + xx)

    def at_x(i):
        return dev((x + i) % NX, y, z, c)

    def at_y(j):
        return dev(x, (y + j) % NY, z, c)

    def at_z(j):
        return dev(x, y, (z + j) % NZ, c)

    sib = dev(x, y, z, 1 - c)

    def push(src, dst, ssem, rsem, to):
        copy = pltpu.make_async_remote_copy(src, dst, ssem, rsem, device_id=to, device_id_type=MESH)
        copy.start()
        return copy

    def took(ref, ssem, rsem):
        return pltpu.make_async_remote_copy(ref, ref, ssem, rsem, device_id=sib, device_id_type=MESH)

    sent = []

    own = pltpu.make_async_copy(
        resid.at[:, pl.ds(pl.multiple_of(c * HALF, 128), HALF)], rg.at[x, y], load_sem.at[0])
    own.start()
    enc_load = pltpu.make_async_copy(
        wenc.at[:, pl.ds(pl.multiple_of(c * HALF, 128), HALF)], we.at[0], load_sem.at[1])
    enc_load.start()
    dec_load = [
        pltpu.make_async_copy(wdec.at[:, q * Q:(q + 1) * Q], wd.at[q], load_sem.at[2 + q]) for q in range(4)
    ]
    for copy in dec_load:
        copy.start()
    bias_load = [
        pltpu.make_async_copy(benc, bo, load_sem.at[6]),
        pltpu.make_async_copy(bdec, bd, load_sem.at[7]),
    ]
    for copy in bias_load:
        copy.start()

    barrier = pltpu.get_barrier_semaphore()
    partners = [at_x(i) for i in (1, 2, 3)] + [at_y(j) for j in NEAR] + [at_z(j) for j in NEAR] + [sib]
    for p in partners:
        pl.semaphore_signal(barrier, 1, device_id=p, device_id_type=MESH)
    own.wait()
    pl.semaphore_wait(barrier, len(partners))

    for j in NEAR:
        push(rg.at[x, y], rg.at[x, y], gsend.at[0], gy.at[y], at_y(j))
    for i in (2, 1, 3):
        push(rg.at[x, y], rg.at[x, y], gsend.at[1], gx.at[x], at_x(i))
    def pass_on(n, carry):
        yy = (y + near_step(n)) % NY
        took(rg.at[x, yy], gsend.at[0], gy.at[yy]).wait_recv()
        for i in (2, 1, 3):
            push(rg.at[x, yy], rg.at[x, yy], gsend.at[1], gx.at[x], at_x(i))
        return carry

    lax.fori_loop(0, 7, pass_on, 0)
    to_sib = [
        push(wenc.at[:, pl.ds(pl.multiple_of((1 - c) * HALF, 128), HALF)], we.at[1],
             sib_send.at[0], sib_recv.at[0], sib),
        push(benc, bs, sib_send.at[1], sib_recv.at[1], sib),
    ]
    for hh in range(2):
        to_sib.append(
            push(wdec.at[:, pl.ds(pl.multiple_of((2 * (1 - c) + hh) * Q, 128), Q)], wds.at[hh],
                 sib_send.at[2 + hh], sib_recv.at[2 + hh], sib))
    sent.append(took(rg.at[0, pl.ds(0, 7)], gsend.at[0], gy.at[0]))
    sent.append(took(rg.at[pl.ds(0, 3)], gsend.at[1], gx.at[0]))
    sent.extend(to_sib)

    for copy in dec_load:
        copy.wait()
    norm2 = jnp.zeros((LAT, 1), F32)
    for q in range(4):
        w = wd[q].astype(F32)
        norm2 = norm2 + jnp.sum(w * w, axis=1, keepdims=True)
    norm_col = jnp.sqrt(norm2 + epsilon)
    norm_row = jnp.transpose(jnp.broadcast_to(norm_col, (LAT, 128)))[0:1, :]

    enc_load.wait()

    def lay(kk):
        even, odd = rg[2 * kk].astype(F32), rg[2 * kk + 1].astype(F32)
        lhs[:, kk] = jnp.concatenate([even, odd], axis=1).astype(BF16)

    beside_x = x + 1 - 2 * h
    took(rg.at[beside_x], gsend.at[1], gx.at[beside_x]).wait_recv()
    lay(k)
    for kk in range(2):
        xx = 2 * (1 - k) + kk
        took(rg.at[xx], gsend.at[1], gx.at[xx]).wait_recv()
    lay(1 - k)
    to_sib[0].wait_recv()
    to_sib[1].wait_recv()
    rows = lhs[...].reshape(ROWS, HALF)
    for copy in bias_load:
        copy.wait()
    contract = (((1,), (1,)), ((), ()))
    for o in range(2):
        px[o] = lax.dot_general(rows, we[o], contract, preferred_element_type=F32)
    pre_copy = push(px, pr, pr_sem.at[0], pr_sem.at[1], sib)
    sent.append(pre_copy)
    pre_copy.wait_recv()
    cc[0] = jnp.maximum(px[0] + pr[1] + bo[...], 0.0).astype(BF16)
    cc[1] = jnp.maximum(px[1] + pr[0] + bs[...], 0.0).astype(BF16)

    for hh in range(2):
        to_sib[2 + hh].wait_recv()

    def decode(hq):
        total = jnp.dot(cc[0], wd[2 * c + hq], preferred_element_type=F32)
        total = total + jnp.dot(cc[1], wds[hq], preferred_element_type=F32)
        part[hq] = total.astype(BF16).reshape(NY, 2, 8, Q)

    decode(1 - h)

    def scatter_odd(n, carry):
        yy = (y + far_step(n)) % NY
        for kk in range(2):
            xx = 2 * kk + 1 - h
            slot = (xx - x + NX) % NX - 1
            push(part.at[1 - h, yy, kk], got.at[yy, slot], rsend.at[0], rx.at[yy], dev(xx, y, z, c))
        return carry

    lax.fori_loop(0, NY, scatter_odd, 0)
    decode(h)

    def scatter_even(n, carry):
        yy = (y + far_step(n)) % NY
        push(part.at[h, yy, 1 - k], got.at[yy, 1], rsend.at[0], rx.at[yy], at_x(2))
        return carry

    lax.fori_loop(0, NY, scatter_even, 0)
    sent.append(took(got, rsend.at[0], rx.at[0]))

    codes_f32 = cc[0].astype(F32)
    sums_row = jnp.sum(codes_f32, axis=0, keepdims=True)
    sums_col = jnp.transpose(jnp.broadcast_to(sums_row, (128, LAT)))[:, 0:1]
    pbx[x] = jnp.broadcast_to(jnp.sum(sums_row * norm_row), (8, 128))
    for i in (1, 2, 3):
        push(pbx.at[x], pbx.at[x], pen_send.at[0], pen_recv.at[0], at_x(i))
    sent.append(took(pbx.at[pl.ds(0, 3)], pen_send.at[0], pen_recv.at[0]))

    def piece_sum(yy):
        total = part[h, yy, k].astype(F32)
        for i in range(3):
            total = total + got[yy, i].astype(F32)
        return total

    def scatter_y(n, carry):
        step = far_step(n)
        yy = (y + step) % NY
        took(got.at[yy], rsend.at[0], rx.at[yy]).wait_recv()
        mid[yy] = piece_sum(yy).astype(BF16)
        push(mid.at[yy], ups.at[step - 1], rsend.at[1], ry.at[0], at_y(step))
        return carry

    lax.fori_loop(0, 7, scatter_y, 0)
    sent.append(took(ups, rsend.at[1], ry.at[0]))
    took(pbx.at[pl.ds(0, 3)], pen_send.at[0], pen_recv.at[0]).wait_recv()
    pbx_sum = pbx[0] + pbx[1] + pbx[2] + pbx[3]
    pby[y] = pbx_sum
    for j in FAR:
        push(pby.at[y], pby.at[y], pen_send.at[1], pen_recv.at[1], at_y(j))
    sent.append(took(pby.at[pl.ds(0, 7)], pen_send.at[1], pen_recv.at[1]))
    took(got.at[y], rsend.at[0], rx.at[y]).wait_recv()
    acc = piece_sum(y)
    took(ups, rsend.at[1], ry.at[0]).wait_recv()
    for j in range(7):
        acc = acc + ups[j].astype(F32)
    zb[z] = acc.astype(BF16)
    for j in FAR:
        push(zb.at[z], zb.at[z], rsend.at[2], rz.at[0], at_z(j))
    sent.append(took(zb.at[pl.ds(0, 7)], rsend.at[2], rz.at[0]))

    cols = pl.ds(pl.multiple_of(h * Q, 128), Q)
    rows8 = jnp.concatenate([rg[2 * k, y, :, cols].astype(F32), rg[2 * k + 1, y, :, cols].astype(F32)], axis=0)
    first = (2 * c + h) * 7
    bias = jnp.concatenate([bd[pl.ds(first + i, 1), :] for i in range(7)], axis=1)
    took(zb.at[pl.ds(0, 7)], rsend.at[2], rz.at[0]).wait_recv()
    total = zb[0].astype(F32)
    for j in range(1, NZ):
        total = total + zb[j].astype(F32)
    piece = total + bias
    err[c, x, y] = (piece - rows8).astype(BF16)
    rc[c, h] = piece
    for j in NEAR:
        push(err.at[c, x, y], err.at[c, x, y], esend.at[0], ey.at[y], at_y(j))
    for i in (2, 1, 3):
        push(err.at[c, x, y], err.at[c, x, y], esend.at[1], ex.at[x], at_x(i))
    beside = dev(x + 1 - 2 * h, y, z, c)
    push(rc.at[c, h], rc.at[c, h], rc_sem.at[0], rc_sem.at[1], beside)
    sent.append(took(rc.at[0, 0], rc_sem.at[0], rc_sem.at[1]))
    took(pby.at[pl.ds(0, 7)], pen_send.at[1], pen_recv.at[1]).wait_recv()
    pen = pby[0]
    for j in range(1, NY):
        pen = pen + pby[j]
    pbz[z] = pen
    for j in FAR:
        push(pbz.at[z], pbz.at[z], pen_send.at[2], pen_recv.at[2], at_z(j))
    sent.append(took(pbz.at[pl.ds(0, 7)], pen_send.at[2], pen_recv.at[2]))

    def pass_err(n, carry):
        yy = (y + near_step(n)) % NY
        took(err.at[c, x, yy], esend.at[0], ey.at[yy]).wait_recv()
        for i in (2, 1, 3):
            push(err.at[c, x, yy], err.at[c, x, yy], esend.at[1], ex.at[x], at_x(i))
        return carry

    lax.fori_loop(0, 7, pass_err, 0)
    sent.append(took(err.at[0, 0, pl.ds(0, 7)], esend.at[0], ey.at[0]))
    sent.append(took(err.at[0, pl.ds(0, 3)], esend.at[1], ex.at[0]))
    push(err.at[c, x], err.at[c, x], esend.at[2], es.at[x], sib)
    took(rc.at[c, h], rc_sem.at[0], rc_sem.at[1]).wait_recv()
    push(rc.at[c], rc.at[c], rc_sem.at[2], rc_sem.at[3], sib)
    sent.append(took(rc.at[0], rc_sem.at[2], rc_sem.at[3]))
    took(pbz.at[pl.ds(0, 7)], pen_send.at[2], pen_recv.at[2]).wait_recv()
    pen = pbz[0]
    for j in range(1, NZ):
        pen = pen + pbz[j]
    pbc[c] = pen
    push(pbc.at[c], pbc.at[c], pen_send.at[3], pen_recv.at[3], sib)
    sent.append(took(pbc.at[0], pen_send.at[3], pen_recv.at[3]))
    for i in (1, 3, 2):
        xx = (x + i) % NX
        took(err.at[c, xx], esend.at[1], ex.at[xx]).wait_recv()
        push(err.at[c, xx], err.at[c, xx], esend.at[2], es.at[xx], sib)
    sent.append(took(err.at[0], esend.at[2], es.at[0]))

    codes = cc[0]
    ratio = sums_col / norm_col

    def quarter(co, hq, cg):
        q = 2 * co + hq
        e = jnp.stack([err[co, hq], err[co, 2 + hq]], axis=1).reshape(ROWS, Q)
        w = wd[q]
        grad = lax.dot_general(codes, e, (((0,), (0,)), ((), ())), preferred_element_type=F32)
        gw_o[q] = (grad + ratio * w.astype(F32)).astype(BF16)
        sums = jnp.sum(e.astype(F32), axis=0, keepdims=True)
        for i in range(7):
            gb_o[pl.ds(7 * q + i, 1), :] = sums[:, i * 128:(i + 1) * 128]
        return cg + lax.dot_general(w, e, contract, preferred_element_type=F32)

    cg = jnp.zeros((LAT, ROWS), F32)
    cg = quarter(c, h, cg)
    cg = quarter(c, 1 - h, cg)
    for hq in (1 - h, h):
        for kk in range(2):
            xx = 2 * kk + hq
            took(err.at[1 - c, xx], esend.at[2], es.at[xx]).wait_recv()
        cg = quarter(1 - c, hq, cg)
    cg_o[...] = cg + norm_col

    squares = jnp.zeros((8, Q), F32)
    for co in range(2):
        for xx in range(NX):
            e = err[co, xx].astype(F32)
            squares = squares + jnp.sum(e * e, axis=0)
    took(pbc.at[c], pen_send.at[3], pen_recv.at[3]).wait_recv()
    loss_o[...] = (0.5 * jnp.sum(squares) + (pbc[0] + pbc[1])) * SCALE

    took(rc.at[c], rc_sem.at[2], rc_sem.at[3]).wait_recv()
    for co in range(2):
        for hq in range(2):
            q = 2 * co + hq
            v = rc[co, hq]
            recon_o[:, q * Q:(q + 1) * Q] = jnp.where(h == 0, v[0:4], v[4:8])

    for copy in sent:
        copy.wait_send()


def write_out(recon, grad, code_grad, bias_grad, loss, recon_o, grad_o, code_grad_o, bias_grad_o, loss_o, sem):
    copies = [pltpu.make_async_copy(grad.at[q], grad_o.at[:, q * Q:(q + 1) * Q], sem.at[q]) for q in range(4)]
    copies += [
        pltpu.make_async_copy(recon, recon_o, sem.at[4]),
        pltpu.make_async_copy(code_grad, code_grad_o, sem.at[5]),
        pltpu.make_async_copy(bias_grad, bias_grad_o, sem.at[6]),
    ]
    for copy in copies:
        copy.start()
    loss_o[...] = loss[0:1, 0:1]
    for copy in copies:
        copy.wait()


def per_device(resid, w_enc, b_enc, w_dec, b_dec):
    hbm = pl.BlockSpec(memory_space=pltpu.HBM)
    vmem = pl.BlockSpec(memory_space=pltpu.VMEM)
    dma = pltpu.SemaphoreType.DMA
    made = pl.pallas_call(
        kernel,
        out_shape=(
            jax.ShapeDtypeStruct((4, D), F32),
            jax.ShapeDtypeStruct((4, LAT, Q), BF16),
            jax.ShapeDtypeStruct((LAT, ROWS), F32),
            jax.ShapeDtypeStruct((28, 128), F32),
            jax.ShapeDtypeStruct((8, 128), F32),
        ),
        in_specs=[hbm] * 5,
        out_specs=(vmem,) * 5,
        scratch_shapes=[
            pltpu.VMEM((NX, NY, 4, HALF), BF16),
            pltpu.VMEM((2, LAT, HALF), BF16),
            pltpu.VMEM((4, LAT, Q), BF16),
            pltpu.VMEM((2, LAT, Q), BF16),
            pltpu.VMEM((1, LAT), F32),
            pltpu.VMEM((1, LAT), F32),
            pltpu.VMEM((28, 128), F32),
            pltpu.VMEM((NY, 2, 8, HALF), BF16),
            pltpu.VMEM((2, ROWS, LAT), F32),
            pltpu.VMEM((2, ROWS, LAT), F32),
            pltpu.VMEM((2, ROWS, LAT), BF16),
            pltpu.VMEM((2, NY, 2, 8, Q), BF16),
            pltpu.VMEM((NY, 3, 8, Q), BF16),
            pltpu.VMEM((NY, 8, Q), BF16),
            pltpu.VMEM((7, 8, Q), BF16),
            pltpu.VMEM((NZ, 8, Q), BF16),
            pltpu.VMEM((2, NX, NY, 8, Q), BF16),
            pltpu.VMEM((2, 2, 8, Q), F32),
            pltpu.VMEM((NX, 8, 128), F32),
            pltpu.VMEM((NY, 8, 128), F32),
            pltpu.VMEM((NZ, 8, 128), F32),
            pltpu.VMEM((2, 8, 128), F32),
            dma((8,)),
            dma((NY,)),
            dma((NX,)),
            dma((2,)),
            dma((4,)),
            dma((4,)),
            dma((2,)),
            dma((NY,)),
            dma((1,)),
            dma((1,)),
            dma((3,)),
            dma((NY,)),
            dma((NX,)),
            dma((NX,)),
            dma((3,)),
            dma((4,)),
            dma((4,)),
            dma((4,)),
        ],
        compiler_params=pltpu.CompilerParams(
            collective_id=0, has_side_effects=True, vmem_limit_bytes=48 << 20
        ),
        cost_estimate=pl.CostEstimate(flops=900_000_000, bytes_accessed=6_000_000, transcendentals=0),
    )(*[pltpu.with_memory_space_constraint(v, pltpu.HBM) for v in (resid, w_enc, b_enc.reshape(1, LAT), w_dec, b_dec.reshape(28, 128))])
    recon, grad_w_dec, code_grad, grad_b_dec, loss = pl.pallas_call(
        write_out,
        out_shape=(
            jax.ShapeDtypeStruct((4, D), F32),
            jax.ShapeDtypeStruct((LAT, D), BF16),
            jax.ShapeDtypeStruct((LAT, ROWS), F32),
            jax.ShapeDtypeStruct((28, 128), F32),
            jax.ShapeDtypeStruct((1, 1), F32),
        ),
        in_specs=[vmem] * 5,
        out_specs=(hbm,) * 4 + (vmem,),
        scratch_shapes=[dma((7,))],
        compiler_params=pltpu.CompilerParams(vmem_limit_bytes=1 << 20),
    )(*made)
    return recon, grad_w_dec, code_grad.T, grad_b_dec.reshape(D), loss.reshape(())


def solution(mesh):
    in_specs = (
        P("tensor", None),
        P(("section", "tensor"), None),
        P(("section", "tensor")),
        P(("section", "tensor"), None),
        P(),
    )
    out_specs = (
        P("tensor", None),
        P(("section", "tensor"), None),
        P(None, ("section", "tensor")),
        P(),
        P(),
    )
    return jax.shard_map(
        per_device, mesh=mesh, in_specs=in_specs, out_specs=out_specs, check_vma=False
    )
```

```python
import functools

import jax
import jax.numpy as jnp
from jax import lax
from jax.experimental import pallas as pl
from jax.experimental.pallas import tpu as pltpu
from jax.sharding import PartitionSpec as P

MESH = pl.DeviceIdType.MESH
F32, BF16 = jnp.float32, jnp.bfloat16
epsilon = 1e-06

NX, NY, NZ = 4, 8, 8
D, LAT, ROWS = 3584, 224, 128
HALF, Q = D // 2, D // 4
SCALE = 1.0 / (ROWS * D)
NEAR = (1, 7, 2, 6, 3, 5, 4)
FAR = (4, 3, 5, 2, 6, 1, 7)


def far_step(n):
    return 4 + (1 - 2 * (n % 2)) * ((n + 1) // 2)


def near_step(n):
    return (1 - 2 * (n % 2)) * ((n + 2) // 2) + 8 * (n % 2)


def kernel(
    resid, wenc, benc, wdec, bdec,
    recon_o, gw_o, cg_o, gb_o, loss_o,
    rg, we, wd, wds, bo, bs, bd, lhs, px, pr, cc, part, got, mid, ups, zb, err, rc,
    pbx, pby, pbz, pbc,
    load_sem, gy, gx, gsend, sib_send, sib_recv, pr_sem,
    rx, ry, rz, rsend, ey, ex, es, esend, rc_sem, pen_recv, pen_send,
):
    section, tensor = lax.axis_index("section"), lax.axis_index("tensor")
    z, c = section // 2, section % 2
    y, x = tensor // 4, tensor % 4
    h, k = x % 2, x // 2

    def dev(xx, yy, zz, co):
        return (zz * 2 + co, yy * 4 + xx)

    def at_x(i):
        return dev((x + i) % NX, y, z, c)

    def at_y(j):
        return dev(x, (y + j) % NY, z, c)

    def at_z(j):
        return dev(x, y, (z + j) % NZ, c)

    sib = dev(x, y, z, 1 - c)

    def push(src, dst, ssem, rsem, to):
        copy = pltpu.make_async_remote_copy(src, dst, ssem, rsem, device_id=to, device_id_type=MESH)
        copy.start()
        return copy

    def took(ref, ssem, rsem):
        return pltpu.make_async_remote_copy(ref, ref, ssem, rsem, device_id=sib, device_id_type=MESH)

    sent = []

    own = pltpu.make_async_copy(
        resid.at[:, pl.ds(pl.multiple_of(c * HALF, 128), HALF)], rg.at[x, y], load_sem.at[0])
    own.start()
    enc_load = pltpu.make_async_copy(
        wenc.at[:, pl.ds(pl.multiple_of(c * HALF, 128), HALF)], we.at[0], load_sem.at[1])
    enc_load.start()
    dec_load = [
        pltpu.make_async_copy(wdec.at[:, q * Q:(q + 1) * Q], wd.at[q], load_sem.at[2 + q]) for q in range(4)
    ]
    for copy in dec_load:
        copy.start()
    bias_load = [
        pltpu.make_async_copy(benc, bo, load_sem.at[6]),
        pltpu.make_async_copy(bdec, bd, load_sem.at[7]),
    ]
    for copy in bias_load:
        copy.start()

    barrier = pltpu.get_barrier_semaphore()
    partners = [at_x(i) for i in (1, 2, 3)] + [at_y(j) for j in NEAR] + [at_z(j) for j in NEAR] + [sib]
    for p in partners:
        pl.semaphore_signal(barrier, 1, device_id=p, device_id_type=MESH)
    own.wait()
    pl.semaphore_wait(barrier, len(partners))

    for j in FAR:
        push(rg.at[x, y], rg.at[x, y], gsend.at[0], gy.at[y], at_y(j))
    for i in (2, 1, 3):
        push(rg.at[x, y], rg.at[x, y], gsend.at[1], gx.at[x], at_x(i))
    def pass_on(n, carry):
        yy = (y + near_step(n)) % NY
        took(rg.at[x, yy], gsend.at[0], gy.at[yy]).wait_recv()
        for i in (2, 1, 3):
            push(rg.at[x, yy], rg.at[x, yy], gsend.at[1], gx.at[x], at_x(i))
        return carry

    lax.fori_loop(0, 7, pass_on, 0)
    to_sib = [
        push(wenc.at[:, pl.ds(pl.multiple_of((1 - c) * HALF, 128), HALF)], we.at[1],
             sib_send.at[0], sib_recv.at[0], sib),
        push(benc, bs, sib_send.at[1], sib_recv.at[1], sib),
    ]
    for hh in range(2):
        to_sib.append(
            push(wdec.at[:, pl.ds(pl.multiple_of((2 * (1 - c) + hh) * Q, 128), Q)], wds.at[hh],
                 sib_send.at[2 + hh], sib_recv.at[2 + hh], sib))
    sent.append(took(rg.at[0, pl.ds(0, 7)], gsend.at[0], gy.at[0]))
    sent.append(took(rg.at[pl.ds(0, 3)], gsend.at[1], gx.at[0]))
    sent.extend(to_sib)

    for copy in dec_load:
        copy.wait()
    norm2 = jnp.zeros((LAT, 1), F32)
    for q in range(4):
        w = wd[q].astype(F32)
        norm2 = norm2 + jnp.sum(w * w, axis=1, keepdims=True)
    norm_col = jnp.sqrt(norm2 + epsilon)
    norm_row = jnp.transpose(jnp.broadcast_to(norm_col, (LAT, 128)))[0:1, :]

    enc_load.wait()

    def lay(kk):
        even, odd = rg[2 * kk].astype(F32), rg[2 * kk + 1].astype(F32)
        lhs[:, kk] = jnp.concatenate([even, odd], axis=1).astype(BF16)

    beside_x = x + 1 - 2 * h
    took(rg.at[beside_x], gsend.at[1], gx.at[beside_x]).wait_recv()
    lay(k)
    for kk in range(2):
        xx = 2 * (1 - k) + kk
        took(rg.at[xx], gsend.at[1], gx.at[xx]).wait_recv()
    lay(1 - k)
    to_sib[0].wait_recv()
    to_sib[1].wait_recv()
    rows = lhs[...].reshape(ROWS, HALF)
    for copy in bias_load:
        copy.wait()
    contract = (((1,), (1,)), ((), ()))
    for o in range(2):
        px[o] = lax.dot_general(rows, we[o], contract, preferred_element_type=F32)
    pre_copy = push(px, pr, pr_sem.at[0], pr_sem.at[1], sib)
    sent.append(pre_copy)
    pre_copy.wait_recv()
    cc[0] = jnp.maximum(px[0] + pr[1] + bo[...], 0.0).astype(BF16)
    cc[1] = jnp.maximum(px[1] + pr[0] + bs[...], 0.0).astype(BF16)

    for hh in range(2):
        to_sib[2 + hh].wait_recv()

    def decode(hq):
        total = jnp.dot(cc[0], wd[2 * c + hq], preferred_element_type=F32)
        total = total + jnp.dot(cc[1], wds[hq], preferred_element_type=F32)
        part[hq] = total.astype(BF16).reshape(NY, 2, 8, Q)

    decode(1 - h)

    def scatter_odd(n, carry):
        yy = (y + far_step(n)) % NY
        for kk in range(2):
            xx = 2 * kk + 1 - h
            slot = (xx - x + NX) % NX - 1
            push(part.at[1 - h, yy, kk], got.at[yy, slot], rsend.at[0], rx.at[yy], dev(xx, y, z, c))
        return carry

    lax.fori_loop(0, NY, scatter_odd, 0)
    decode(h)

    def scatter_even(n, carry):
        yy = (y + far_step(n)) % NY
        push(part.at[h, yy, 1 - k], got.at[yy, 1], rsend.at[0], rx.at[yy], at_x(2))
        return carry

    lax.fori_loop(0, NY, scatter_even, 0)
    sent.append(took(got, rsend.at[0], rx.at[0]))

    codes_f32 = cc[0].astype(F32)
    sums_row = jnp.sum(codes_f32, axis=0, keepdims=True)
    sums_col = jnp.transpose(jnp.broadcast_to(sums_row, (128, LAT)))[:, 0:1]
    pbx[x] = jnp.broadcast_to(jnp.sum(sums_row * norm_row), (8, 128))
    for i in (1, 2, 3):
        push(pbx.at[x], pbx.at[x], pen_send.at[0], pen_recv.at[0], at_x(i))
    sent.append(took(pbx.at[pl.ds(0, 3)], pen_send.at[0], pen_recv.at[0]))

    def piece_sum(yy):
        total = part[h, yy, k].astype(F32)
        for i in range(3):
            total = total + got[yy, i].astype(F32)
        return total

    def scatter_y(n, carry):
        step = far_step(n)
        yy = (y + step) % NY
        took(got.at[yy], rsend.at[0], rx.at[yy]).wait_recv()
        mid[yy] = piece_sum(yy).astype(BF16)
        push(mid.at[yy], ups.at[step - 1], rsend.at[1], ry.at[0], at_y(step))
        return carry

    lax.fori_loop(0, 7, scatter_y, 0)
    sent.append(took(ups, rsend.at[1], ry.at[0]))
    took(pbx.at[pl.ds(0, 3)], pen_send.at[0], pen_recv.at[0]).wait_recv()
    pbx_sum = pbx[0] + pbx[1] + pbx[2] + pbx[3]
    pby[y] = pbx_sum
    for j in FAR:
        push(pby.at[y], pby.at[y], pen_send.at[1], pen_recv.at[1], at_y(j))
    sent.append(took(pby.at[pl.ds(0, 7)], pen_send.at[1], pen_recv.at[1]))
    took(got.at[y], rsend.at[0], rx.at[y]).wait_recv()
    acc = piece_sum(y)
    took(ups, rsend.at[1], ry.at[0]).wait_recv()
    for j in range(7):
        acc = acc + ups[j].astype(F32)
    zb[z] = acc.astype(BF16)
    for j in FAR:
        push(zb.at[z], zb.at[z], rsend.at[2], rz.at[0], at_z(j))
    sent.append(took(zb.at[pl.ds(0, 7)], rsend.at[2], rz.at[0]))

    cols = pl.ds(pl.multiple_of(h * Q, 128), Q)
    rows8 = jnp.concatenate([rg[2 * k, y, :, cols].astype(F32), rg[2 * k + 1, y, :, cols].astype(F32)], axis=0)
    first = (2 * c + h) * 7
    bias = jnp.concatenate([bd[pl.ds(first + i, 1), :] for i in range(7)], axis=1)
    took(zb.at[pl.ds(0, 7)], rsend.at[2], rz.at[0]).wait_recv()
    total = zb[0].astype(F32)
    for j in range(1, NZ):
        total = total + zb[j].astype(F32)
    piece = total + bias
    err[c, x, y] = (piece - rows8).astype(BF16)
    rc[c, h] = piece
    for j in NEAR:
        push(err.at[c, x, y], err.at[c, x, y], esend.at[0], ey.at[y], at_y(j))
    for i in (2, 1, 3):
        push(err.at[c, x, y], err.at[c, x, y], esend.at[1], ex.at[x], at_x(i))
    beside = dev(x + 1 - 2 * h, y, z, c)
    push(rc.at[c, h], rc.at[c, h], rc_sem.at[0], rc_sem.at[1], beside)
    sent.append(took(rc.at[0, 0], rc_sem.at[0], rc_sem.at[1]))
    took(pby.at[pl.ds(0, 7)], pen_send.at[1], pen_recv.at[1]).wait_recv()
    pen = pby[0]
    for j in range(1, NY):
        pen = pen + pby[j]
    pbz[z] = pen
    for j in FAR:
        push(pbz.at[z], pbz.at[z], pen_send.at[2], pen_recv.at[2], at_z(j))
    sent.append(took(pbz.at[pl.ds(0, 7)], pen_send.at[2], pen_recv.at[2]))

    def pass_err(n, carry):
        yy = (y + near_step(n)) % NY
        took(err.at[c, x, yy], esend.at[0], ey.at[yy]).wait_recv()
        for i in (2, 1, 3):
            push(err.at[c, x, yy], err.at[c, x, yy], esend.at[1], ex.at[x], at_x(i))
        return carry

    lax.fori_loop(0, 7, pass_err, 0)
    sent.append(took(err.at[0, 0, pl.ds(0, 7)], esend.at[0], ey.at[0]))
    sent.append(took(err.at[0, pl.ds(0, 3)], esend.at[1], ex.at[0]))
    push(err.at[c, x], err.at[c, x], esend.at[2], es.at[x], sib)
    took(rc.at[c, h], rc_sem.at[0], rc_sem.at[1]).wait_recv()
    push(rc.at[c], rc.at[c], rc_sem.at[2], rc_sem.at[3], sib)
    sent.append(took(rc.at[0], rc_sem.at[2], rc_sem.at[3]))
    took(pbz.at[pl.ds(0, 7)], pen_send.at[2], pen_recv.at[2]).wait_recv()
    pen = pbz[0]
    for j in range(1, NZ):
        pen = pen + pbz[j]
    pbc[c] = pen
    push(pbc.at[c], pbc.at[c], pen_send.at[3], pen_recv.at[3], sib)
    sent.append(took(pbc.at[0], pen_send.at[3], pen_recv.at[3]))
    for i in (1, 3, 2):
        xx = (x + i) % NX
        took(err.at[c, xx], esend.at[1], ex.at[xx]).wait_recv()
        push(err.at[c, xx], err.at[c, xx], esend.at[2], es.at[xx], sib)
    sent.append(took(err.at[0], esend.at[2], es.at[0]))

    codes = cc[0]
    ratio = sums_col / norm_col

    def quarter(co, hq, cg):
        q = 2 * co + hq
        e = jnp.stack([err[co, hq], err[co, 2 + hq]], axis=1).reshape(ROWS, Q)
        w = wd[q]
        grad = lax.dot_general(codes, e, (((0,), (0,)), ((), ())), preferred_element_type=F32)
        gw_o[q] = (grad + ratio * w.astype(F32)).astype(BF16)
        sums = jnp.sum(e.astype(F32), axis=0, keepdims=True)
        for i in range(7):
            gb_o[pl.ds(7 * q + i, 1), :] = sums[:, i * 128:(i + 1) * 128]
        return cg + lax.dot_general(w, e, contract, preferred_element_type=F32)

    cg = jnp.zeros((LAT, ROWS), F32)
    cg = quarter(c, h, cg)
    cg = quarter(c, 1 - h, cg)
    for hq in (1 - h, h):
        for kk in range(2):
            xx = 2 * kk + hq
            took(err.at[1 - c, xx], esend.at[2], es.at[xx]).wait_recv()
        cg = quarter(1 - c, hq, cg)
    cg_o[...] = cg + norm_col

    squares = jnp.zeros((8, Q), F32)
    for co in range(2):
        for xx in range(NX):
            e = err[co, xx].astype(F32)
            squares = squares + jnp.sum(e * e, axis=0)
    took(pbc.at[c], pen_send.at[3], pen_recv.at[3]).wait_recv()
    loss_o[...] = (0.5 * jnp.sum(squares) + (pbc[0] + pbc[1])) * SCALE

    took(rc.at[c], rc_sem.at[2], rc_sem.at[3]).wait_recv()
    for co in range(2):
        for hq in range(2):
            q = 2 * co + hq
            v = rc[co, hq]
            recon_o[:, q * Q:(q + 1) * Q] = jnp.where(h == 0, v[0:4], v[4:8])

    for copy in sent:
        copy.wait_send()


def write_out(recon, grad, code_grad, bias_grad, loss, recon_o, grad_o, code_grad_o, bias_grad_o, loss_o, sem):
    copies = [pltpu.make_async_copy(grad.at[q], grad_o.at[:, q * Q:(q + 1) * Q], sem.at[q]) for q in range(4)]
    copies += [
        pltpu.make_async_copy(recon, recon_o, sem.at[4]),
        pltpu.make_async_copy(code_grad, code_grad_o, sem.at[5]),
        pltpu.make_async_copy(bias_grad, bias_grad_o, sem.at[6]),
    ]
    for copy in copies:
        copy.start()
    loss_o[...] = loss[0:1, 0:1]
    for copy in copies:
        copy.wait()


def per_device(resid, w_enc, b_enc, w_dec, b_dec):
    hbm = pl.BlockSpec(memory_space=pltpu.HBM)
    vmem = pl.BlockSpec(memory_space=pltpu.VMEM)
    dma = pltpu.SemaphoreType.DMA
    made = pl.pallas_call(
        kernel,
        out_shape=(
            jax.ShapeDtypeStruct((4, D), F32),
            jax.ShapeDtypeStruct((4, LAT, Q), BF16),
            jax.ShapeDtypeStruct((LAT, ROWS), F32),
            jax.ShapeDtypeStruct((28, 128), F32),
            jax.ShapeDtypeStruct((8, 128), F32),
        ),
        in_specs=[hbm] * 5,
        out_specs=(vmem,) * 5,
        scratch_shapes=[
            pltpu.VMEM((NX, NY, 4, HALF), BF16),
            pltpu.VMEM((2, LAT, HALF), BF16),
            pltpu.VMEM((4, LAT, Q), BF16),
            pltpu.VMEM((2, LAT, Q), BF16),
            pltpu.VMEM((1, LAT), F32),
            pltpu.VMEM((1, LAT), F32),
            pltpu.VMEM((28, 128), F32),
            pltpu.VMEM((NY, 2, 8, HALF), BF16),
            pltpu.VMEM((2, ROWS, LAT), F32),
            pltpu.VMEM((2, ROWS, LAT), F32),
            pltpu.VMEM((2, ROWS, LAT), BF16),
            pltpu.VMEM((2, NY, 2, 8, Q), BF16),
            pltpu.VMEM((NY, 3, 8, Q), BF16),
            pltpu.VMEM((NY, 8, Q), BF16),
            pltpu.VMEM((7, 8, Q), BF16),
            pltpu.VMEM((NZ, 8, Q), BF16),
            pltpu.VMEM((2, NX, NY, 8, Q), BF16),
            pltpu.VMEM((2, 2, 8, Q), F32),
            pltpu.VMEM((NX, 8, 128), F32),
            pltpu.VMEM((NY, 8, 128), F32),
            pltpu.VMEM((NZ, 8, 128), F32),
            pltpu.VMEM((2, 8, 128), F32),
            dma((8,)),
            dma((NY,)),
            dma((NX,)),
            dma((2,)),
            dma((4,)),
            dma((4,)),
            dma((2,)),
            dma((NY,)),
            dma((1,)),
            dma((1,)),
            dma((3,)),
            dma((NY,)),
            dma((NX,)),
            dma((NX,)),
            dma((3,)),
            dma((4,)),
            dma((4,)),
            dma((4,)),
        ],
        compiler_params=pltpu.CompilerParams(
            collective_id=0, has_side_effects=True, vmem_limit_bytes=48 << 20
        ),
        cost_estimate=pl.CostEstimate(flops=900_000_000, bytes_accessed=6_000_000, transcendentals=0),
    )(*[pltpu.with_memory_space_constraint(v, pltpu.HBM) for v in (resid, w_enc, b_enc.reshape(1, LAT), w_dec, b_dec.reshape(28, 128))])
    recon, grad_w_dec, code_grad, grad_b_dec, loss = pl.pallas_call(
        write_out,
        out_shape=(
            jax.ShapeDtypeStruct((4, D), F32),
            jax.ShapeDtypeStruct((LAT, D), BF16),
            jax.ShapeDtypeStruct((LAT, ROWS), F32),
            jax.ShapeDtypeStruct((28, 128), F32),
            jax.ShapeDtypeStruct((1, 1), F32),
        ),
        in_specs=[vmem] * 5,
        out_specs=(hbm,) * 4 + (vmem,),
        scratch_shapes=[dma((7,))],
        compiler_params=pltpu.CompilerParams(vmem_limit_bytes=1 << 20),
    )(*made)
    return recon, grad_w_dec, code_grad.T, grad_b_dec.reshape(D), loss.reshape(())


def solution(mesh):
    in_specs = (
        P("tensor", None),
        P(("section", "tensor"), None),
        P(("section", "tensor")),
        P(("section", "tensor"), None),
        P(),
    )
    out_specs = (
        P("tensor", None),
        P(("section", "tensor"), None),
        P(None, ("section", "tensor")),
        P(),
        P(),
    )
    return jax.shard_map(
        per_device, mesh=mesh, in_specs=in_specs, out_specs=out_specs, check_vma=False
    )
```
